32 devices in a mesh: cols: 8 (over z, core), rep: 4 (over y, x).
Axes of the slice: x: 2, y: 2, z: 4, core: 2. Of those that a mesh axis runs over, the one named last changes fastest.
Arguments:
- hamiltonian_band: float32 [16, 5, 128, 128], P('cols'), may hold values from -0.25 to 0.25
- margin_factors: float32 [16, 256, 128], P('cols', 'rep'), may hold values from -0.25 to 0.25
- neighbour_mask: int32 [16, 5], P('cols'), may hold values from 0 to 1, as said below
- fermi_level: float32 [1], replicated, may hold values from -0.3 to 0.3
Outputs:
- density: float32 [16, 640, 640], P('cols', 'rep')
The draws below stay inside these ranges and needn't reach their ends.
Inputs may be any that keep to these rules, and one draw needn't show every extreme that they name: `neighbour_mask`: entry 2 of every row is 1; every row has 3 to 5 ones; some row has 5 ones and some row has exactly 3.
All inputs are finite; a program needn't handle non-finite values.
Results may differ from the reference program's by a relative error of at most 0.0003.
Values sent between devices are 32-bit elements; how exact they have to be, the bound alone decides.
No kernel may reach another device: no remote copies, remote signals or barrier semaphores. Data moves between devices by JAX's collectives and lax.ppermute only.
A program may use at most 64 MiB of HBM per device.

```python
import jax
import jax.numpy as jnp
from jax import lax

B = 128
P_SIZE = 256
W = 2
ROOT = 2
SIGN = 2
NC = 5
M = 640
NB = 16


def draw_neighbour_mask(key, part):
    key_count, key_order = jax.random.split(jax.random.fold_in(key, 17))
    sides = 2 * W
    extra = jax.random.randint(key_count, (NB,), 2, sides + 1)
    extra = extra.at[0].set(sides).at[1].set(2)
    scores = jax.random.randint(key_order, (NB, sides), 0, 1 << 20) * sides + jnp.arange(sides, dtype=jnp.int32)[None, :]
    ranking = jnp.argsort(jnp.argsort(scores, axis=1, stable=True), axis=1, stable=True)
    chosen = (ranking < extra[:, None]).astype(jnp.int32)
    center = jnp.ones((NB, 1), jnp.int32)
    return jnp.concatenate([chosen[:, :W], center, chosen[:, W:]], axis=1)


def steps_of(key, shape, cuts, least, top_value):
    loudness = 1.0
    for axis_at, parts in cuts:
        draws = jax.random.uniform(jax.random.fold_in(jax.random.fold_in(key, 6), axis_at), (parts,), jnp.float32, least / len(cuts), top_value / len(cuts))
        loudness = loudness * jnp.repeat(jnp.exp(draws), shape[axis_at] // parts).reshape((-1,) + (1,) * (len(shape) - 1 - axis_at))
    return loudness


def centred(own_key, extent, scale, most, cuts=(), kind=jnp.bfloat16):
    array = jax.random.normal(own_key, extent, jnp.float32) * scale
    if len(cuts) > 0:
        array = steps_of(own_key, extent, cuts, -0.22, 0.18) * array
    return jnp.clip(array, min=-most, max=most).astype(kind)


def setup_inputs(seed: int = 0) -> dict:
    arg_keys = jax.random.split(jax.random.key(seed), 5)
    hamiltonian_band = centred(arg_keys[0], (NB, NC, B, B), M ** -0.5, 0.25, ((0, 8),), jnp.float32)
    margin_factors = centred(arg_keys[1], (NB, P_SIZE, B), M ** -0.5, 0.25, ((0, 8), (1, 4)), jnp.float32)
    neighbour_mask = draw_neighbour_mask(jax.random.fold_in(arg_keys[4], 71), 0)
    fermi_level = jnp.clip(jax.random.uniform(arg_keys[3], (1,), jnp.float32, -0.3, 0.3), -0.3, 0.3)
    return dict(hamiltonian_band=hamiltonian_band, margin_factors=margin_factors, neighbour_mask=neighbour_mask, fermi_level=fermi_level)


def matmul(left, right):
    return jnp.dot(left, right, preferred_element_type=jnp.float32, precision=lax.Precision.HIGHEST)

def mirror_blocks(band, mask_row):
    block_rows = []
    for left_idx in range(NC):
        block_line = []
        for right_idx in range(NC):
            if abs(left_idx - right_idx) <= W:
                pair = band[right_idx, left_idx - right_idx + W] + band[left_idx, W - left_idx + right_idx].T
                weight = mask_row[left_idx] * mask_row[right_idx]
                block_line.append(0.5 * pair * weight)
            else:
                block_line.append(jnp.zeros((B, B), jnp.float32))
        block_rows.append(jnp.concatenate(block_line, axis=1))
    return jnp.concatenate(block_rows, axis=0)

def reference(hamiltonian_band, margin_factors, neighbour_mask, fermi_level):
    identity = jnp.eye(M, dtype=jnp.float32)

    def one_column(column_id):
        offsets = jnp.arange(NC, dtype=jnp.int32) - W
        neighbours = ((column_id + offsets) % NB).astype(jnp.int32)
        mask_row = neighbour_mask[column_id].astype(jnp.float32)
        factors = margin_factors[neighbours] * mask_row[:, None, None]
        stacked = jnp.transpose(factors, (1, 0, 2)).reshape(P_SIZE, M)
        margin = identity + matmul(stacked.T, stacked)
        hamilton = mirror_blocks(hamiltonian_band[neighbours], mask_row)
        root_scale = 2.0 * jnp.sqrt(jnp.sum(margin * margin) / M)
        forward_iter = margin / root_scale
        inverse_iter = identity
        for iteration in range(ROOT):
            step_mat = 0.5 * (3.0 * identity - matmul(inverse_iter, forward_iter))
            forward_iter = matmul(forward_iter, step_mat)
            inverse_iter = matmul(inverse_iter, step_mat)
        inverse_iter = inverse_iter / jnp.sqrt(root_scale)
        ortho = matmul(inverse_iter, matmul(hamilton, inverse_iter))
        shifted = ortho - fermi_level[0] * identity
        spread = 2.0 * jnp.sqrt(jnp.sum(shifted * shifted) / M + 1e-05)
        sign_iter = shifted / spread
        for iteration in range(SIGN):
            square_mat = matmul(sign_iter, sign_iter)
            cube_mat = matmul(sign_iter, square_mat)
            sign_iter = 0.5 * (3.0 * sign_iter - cube_mat)
        return 0.5 * (identity - sign_iter)
    return lax.map(one_column, jnp.arange(NB, dtype=jnp.int32))
```

```python
import functools

import jax
import jax.numpy as jnp
from jax import lax
from jax.experimental import pallas as pl
from jax.experimental.pallas import tpu as pltpu
from jax.sharding import PartitionSpec as P

F32 = jnp.float32
BF16 = jnp.bfloat16


def split(value):
    high = value.astype(BF16)
    return high, (value - high.astype(F32)).astype(BF16)


def dot(left, right):
    return jnp.dot(left, right, preferred_element_type=F32)


def dot3(left, right):
    (left_high, left_low), (right_high, right_low) = left, right
    return dot(left_high, right_high) + (dot(left_high, right_low) + dot(left_low, right_high))


def total(value):
    return jnp.sum(jnp.sum(value, axis=0, keepdims=True), axis=1, keepdims=True)


def eye(rows, columns, first=0):
    row = lax.broadcasted_iota(jnp.int32, (rows, columns), 0) + first
    column = lax.broadcasted_iota(jnp.int32, (rows, columns), 1)
    return jnp.where(row == column, 1.0, 0.0).astype(F32)


def kernel(
    cols, reach, rep_size,
    mask, fermi, place,
    m_left, m_own, m_right, h_left, h_own, h_right,
    out,
    ham, ham_h, ham_l, y_h, y_l, yt_h, yt_l, prod, shift, shift_h, shift_l, sq_h, sq_l,
):
    block = m_own.shape[2]
    depth = m_own.shape[1]
    count = 2 * reach + 1
    width = count * block
    window = cols + 2 * reach

    def margin(w):
        if w < reach:
            return m_left[w]
        if w < reach + cols:
            return m_own[w - reach]
        return m_right[w - reach - cols]

    def band(w, e):
        if w < reach:
            return h_left[w, e]
        if w < reach + cols:
            return h_own[w - reach, e]
        return h_right[w - reach - cols, e]

    def at(index):
        return slice(index * block, (index + 1) * block)

    keep = [[mask[c, a].astype(F32) for a in range(count)] for c in range(cols)]

    trace = [jnp.zeros((1, 1), F32) for _ in range(cols)]
    for w in range(window):
        x = margin(w)
        xt = x.T
        x_sq = total(x * x)
        for c in range(cols):
            a = w - c
            if 0 <= a < count:
                m = keep[c][a]
                high, low = split(x * m)
                y_h[c, :, at(a)] = high
                y_l[c, :, at(a)] = low
                high, low = split(xt * m)
                yt_h[c, at(a), :] = high
                yt_l[c, at(a), :] = low
                trace[c] = trace[c] + x_sq * m

    state = []
    small_eye = eye(depth, depth)
    for c in range(cols):
        gram = dot3((y_h[c], y_l[c]), (yt_h[c], yt_l[c]))
        sum_sq = width + 2.0 * trace[c] + total(gram * gram)
        s0 = 1.0 / (2.0 * jnp.sqrt(sum_sq / width))
        t0 = 1.5 - 0.5 * s0
        u0 = 1.5 - 0.5 * t0 * t0 * s0
        u1 = 0.5 * t0 * (t0 - s0)
        u2 = 0.5 * (0.25 * s0 - t0)
        u3 = 0.125
        e1 = -t0 * u1 - 0.5 * u0
        e2 = -t0 * u2 + 0.5 * u1
        e3 = -t0 * u3 + 0.5 * u2
        e4 = 0.5 * u3
        root = jnp.sqrt(s0)
        kappa = gram * s0
        kappa_s = split(kappa)
        square = dot3(kappa_s, kappa_s)
        cube = dot3(kappa_s, split(square))
        poly = (e1 * small_eye + e2 * kappa + e3 * square + e4 * cube) * (s0 * root)
        poly_s = split(poly)
        p = dot3(poly_s, (y_h[c], y_l[c]))
        pt = dot3((yt_h[c], yt_l[c]), poly_s)
        state.append((t0 * u0 * root, split(p), split(pt)))

    for a in range(window):
        for b in range(a + 1):
            if a - b <= reach:
                value = 0.5 * (band(b, a - b + reach) + band(a, reach - a + b).T)
                high, low = split(value)
                ham[at(a), at(b)] = value
                ham_h[at(a), at(b)] = high
                ham_l[at(a), at(b)] = low
                if a != b:
                    value = value.T
                    high, low = split(value)
            else:
                value = jnp.zeros((block, block), F32)
                high = low = jnp.zeros((block, block), BF16)
                ham[at(a), at(b)] = value
                ham_h[at(a), at(b)] = high
                ham_l[at(a), at(b)] = low
            if a != b:
                ham[at(b), at(a)] = value
                ham_h[at(b), at(a)] = high
                ham_l[at(b), at(a)] = low

    rows = width // rep_size
    first = pl.multiple_of(place[0] * rows, rows)
    big_eye = eye(width, width)
    level = fermi[0]
    scale = []
    for c in range(cols):
        z0, p_s, pt_s = state[c]
        here = slice(c * block, c * block + width)
        mask_col = jnp.concatenate([jnp.full((block, 1), keep[c][a], F32) for a in range(count)], axis=0)
        mask_row = jnp.concatenate([jnp.full((1, block), keep[c][a], F32) for a in range(count)], axis=1)
        side = dot3((ham_h[here, here], ham_l[here, here]), (yt_h[c], yt_l[c])) * mask_col
        core = dot3((y_h[c], y_l[c]), split(side))
        factor = z0 * side + 0.5 * dot3(pt_s, split(core))
        prod[c] = dot3(split(factor), p_s)
        energy = prod[c] + prod[c].T + (ham[here, here] * (z0 * z0 * mask_col)) * mask_row - level * big_eye
        shift[c] = energy
        high, low = split(energy)
        shift_h[c] = high
        shift_l[c] = low
        spread_sq = 4.0 * (total(energy * energy) / width + 1e-05)
        scale.append(1.0 / spread_sq)

    for c in range(cols):
        prod[c] = dot(shift_h[c], shift_l[c])
        square = (dot(shift_h[c], shift_h[c]) + (prod[c] + prod[c].T)) * scale[c]
        high, low = split(square)
        sq_h[c] = high
        sq_l[c] = low

    part_eye = eye(rows, width, first)
    for c in range(cols):
        sq_s = (sq_h[c], sq_l[c])
        x0 = shift[c, pl.ds(first, rows), :] * jnp.sqrt(scale[c])
        x1 = 1.5 * x0 - 0.5 * dot3(split(x0), sq_s)
        y1 = 1.5 * x1 - 0.5 * dot3(split(x1), sq_s)
        y2 = 1.5 * y1 - 0.5 * dot3(split(y1), sq_s)
        y3 = dot3(split(y2), sq_s)
        out[c] = 0.5 * (part_eye - (1.5 * x1 - 0.5 * y3))


def extended(value, reach):
    count = lax.axis_size("cols")
    forward = [(i, (i + 1) % count) for i in range(count)]
    backward = [(target, source) for source, target in forward]
    size = value.shape[0]
    low = lax.ppermute(lax.slice_in_dim(value, size - reach, size, axis=0), "cols", forward)
    high = lax.ppermute(lax.slice_in_dim(value, 0, reach, axis=0), "cols", backward)
    return low, high


def on_device(hamiltonian_band, margin_factors, neighbour_mask, fermi_level):
    cols, count, block, _ = hamiltonian_band.shape
    reach = (count - 1) // 2
    width = count * block
    rep_size = lax.axis_size("rep")
    rows = width // rep_size
    h_left, h_right = extended(hamiltonian_band, reach)
    factors = lax.all_gather(margin_factors, "rep", axis=1, tiled=True)
    m_left, m_right = extended(factors, reach)
    place = lax.axis_index("rep").astype(jnp.int32).reshape(1)
    depth = factors.shape[1]
    window = (cols + 2 * reach) * block
    smem = pl.BlockSpec(memory_space=pltpu.SMEM)
    vmem = pl.BlockSpec(memory_space=pltpu.VMEM)
    return pl.pallas_call(
        functools.partial(kernel, cols, reach, rep_size),
        out_shape=jax.ShapeDtypeStruct((cols, rows, width), F32),
        in_specs=[smem] * 3 + [vmem] * 6,
        out_specs=vmem,
        scratch_shapes=[
            pltpu.VMEM((window, window), F32),
            pltpu.VMEM((window, window), BF16),
            pltpu.VMEM((window, window), BF16),
            pltpu.VMEM((cols, depth, width), BF16),
            pltpu.VMEM((cols, depth, width), BF16),
            pltpu.VMEM((cols, width, depth), BF16),
            pltpu.VMEM((cols, width, depth), BF16),
            pltpu.VMEM((cols, width, width), F32),
            pltpu.VMEM((cols, width, width), F32),
            pltpu.VMEM((cols, width, width), BF16),
            pltpu.VMEM((cols, width, width), BF16),
            pltpu.VMEM((cols, width, width), BF16),
            pltpu.VMEM((cols, width, width), BF16),
        ],
        compiler_params=pltpu.CompilerParams(vmem_limit_bytes=48 * 2**20),
    )(neighbour_mask, fermi_level, place, m_left, factors, m_right, h_left, hamiltonian_band, h_right)


def solution(mesh):
    in_specs = (P("cols", None, None, None), P("cols", "rep", None), P("cols", None), P())
    out_specs = P("cols", "rep", None)
    return jax.shard_map(
        on_device, mesh=mesh, in_specs=in_specs, out_specs=out_specs, check_vma=False
    )
```

```python
import functools

import jax
import jax.numpy as jnp
from jax import lax
from jax.experimental import pallas as pl
from jax.experimental.pallas import tpu as pltpu
from jax.sharding import PartitionSpec as P

F32 = jnp.float32
BF16 = jnp.bfloat16
PACKED = 16


def split(value):
    high = value.astype(BF16)
    return high, (value - high.astype(F32)).astype(BF16)


def dot(left, right):
    return jnp.dot(left, right, preferred_element_type=F32)


def dot3(left, right):
    (left_high, left_low), (right_high, right_low) = left, right
    return dot(
        jnp.concatenate([left_high, left_low, left_high], axis=1),
        jnp.concatenate([right_high, right_high, right_low], axis=0),
    )


def total(value):
    return jnp.sum(jnp.sum(value, axis=0, keepdims=True), axis=1, keepdims=True)


def eye(rows, columns, first=0):
    row = lax.broadcasted_iota(jnp.int32, (rows, columns), 0) + first
    column = lax.broadcasted_iota(jnp.int32, (rows, columns), 1)
    return jnp.where(row == column, 1.0, 0.0).astype(F32)


def kernel(
    cols, reach, rep_size,
    mask, fermi, place,
    m_left, m_own, m_right, h_left, h_own, h_right,
    out,
    ham, ham_h, ham_l, y_h, y_l, yt_h, yt_l, prod, shift_h, shift_l, sq_h, sq_l, side_h, side_l, whole,
):
    block = m_own.shape[2]
    depth = m_own.shape[1]
    count = 2 * reach + 1
    width = count * block
    window = cols + 2 * reach
    rows = width // rep_size
    columns = range(cols)

    def margin(w):
        if w < reach:
            return m_left[w]
        if w < reach + cols:
            return m_own[w - reach]
        return m_right[w - reach - cols]

    def band(w, e):
        if w < reach:
            return h_left[w, e]
        if w < reach + cols:
            return h_own[w - reach, e]
        return h_right[w - reach - cols, e]

    def at(index):
        return slice(index * block, (index + 1) * block)

    keep = [[mask[c, a].astype(F32) for a in range(count)] for c in columns]

    trace = [jnp.zeros((1, 1), F32) for _ in columns]
    for w in range(window):
        x = margin(w)
        xt = x.T
        x_sq = total(x * x)
        for c in columns:
            a = w - c
            if 0 <= a < count:
                m = keep[c][a]
                y_h[c, :, at(a)], y_l[c, :, at(a)] = split(x * m)
                yt_h[c, at(a), :], yt_l[c, at(a), :] = split(xt * m)
                trace[c] = trace[c] + x_sq * m

    for a in range(window):
        for b in range(a + 1):
            if a - b <= reach:
                value = 0.5 * (band(b, a - b + reach) + band(a, reach - a + b).T)
                ham[at(a), at(b)] = value
                ham_h[at(a), at(b)], ham_l[at(a), at(b)] = split(value)
                if a != b:
                    value = value.T
                    ham[at(b), at(a)] = value
                    ham_h[at(b), at(a)], ham_l[at(b), at(a)] = split(value)
            else:
                none = jnp.zeros((block, block), BF16)
                for i, j in ((a, b), (b, a)):
                    ham_h[at(i), at(j)] = none
                    ham_l[at(i), at(j)] = none

    small_eye = eye(depth, depth)
    gram = [dot3((y_h[c], y_l[c]), (yt_h[c], yt_l[c])) for c in columns]
    coef = []
    kappa = []
    for c in columns:
        sum_sq = width + 2.0 * trace[c] + total(gram[c] * gram[c])
        s0 = 1.0 / (2.0 * jnp.sqrt(sum_sq / width))
        t0 = 1.5 - 0.5 * s0
        u0 = 1.5 - 0.5 * t0 * t0 * s0
        u1 = 0.5 * t0 * (t0 - s0)
        u2 = 0.5 * (0.25 * s0 - t0)
        u3 = 0.125
        root = jnp.sqrt(s0)
        factor = s0 * root
        e1 = (-t0 * u1 - 0.5 * u0) * factor
        e2 = (-t0 * u2 + 0.5 * u1) * factor
        e3 = (-t0 * u3 + 0.5 * u2) * factor
        e4 = 0.5 * u3 * factor
        coef.append((t0 * u0 * root, e1, e2, e3, e4))
        kappa.append(gram[c] * s0)
    kappa_s = [split(kappa[c]) for c in columns]
    square = [dot3(kappa_s[c], kappa_s[c]) for c in columns]
    cube = [dot3(kappa_s[c], split(square[c])) for c in columns]
    poly = []
    for c in columns:
        _, e1, e2, e3, e4 = coef[c]
        poly.append(e1 * small_eye + e2 * kappa[c] + e3 * square[c] + e4 * cube[c])
    poly_s = [split(poly[c]) for c in columns]

    core = []
    for c in columns:
        here = slice(c * block, c * block + width)
        side = dot3((ham_h[here, here], ham_l[here, here]), (yt_h[c], yt_l[c]))
        for a in range(count):
            side_h[c, at(a), :], side_l[c, at(a), :] = split(side[at(a)] * keep[c][a])
    for c in columns:
        core.append(dot3((y_h[c], y_l[c]), (side_h[c], side_l[c])))

    core = [dot3(poly_s[c], split(core[c])) for c in columns]
    core = [dot3(split(core[c]), poly_s[c]) for c in columns]
    factor = []
    for c in columns:
        left = tuple(
            jnp.concatenate(pair, axis=1) for pair in ((side_h[c], yt_h[c]), (side_l[c], yt_l[c]))
        )
        right = split(jnp.concatenate([coef[c][0] * poly[c], 0.5 * core[c]], axis=0))
        factor.append(split(dot3(left, right)))
    for c in columns:
        prod[c] = dot3(factor[c], (y_h[c], y_l[c]))

    level = fermi[0] * eye(block, block)
    scale = []
    for c in columns:
        z0_sq = coef[c][0] * coef[c][0]
        sum_sq = jnp.zeros((block, block), F32)
        for a in range(count):
            for b in range(count):
                value = prod[c, at(a), at(b)] + prod[c, at(b), at(a)].T
                if abs(a - b) <= reach:
                    value = value + ham[at(c + a), at(c + b)] * (z0_sq * (keep[c][a] * keep[c][b]))
                if a == b:
                    value = value - level
                sum_sq = sum_sq + value * value
                if rows % PACKED:
                    whole[c, at(a), at(b)] = value
                high = value.astype(BF16)
                shift_h[c, at(a), at(b)] = high
                shift_l[c, at(a), at(b)] = (2.0 * (value - high.astype(F32))).astype(BF16)
        scale.append(1.0 / (4.0 * (total(sum_sq) / width + 1e-05)))

    for c in columns:
        high = shift_h[c]
        prod[c] = dot(
            jnp.concatenate([high, high], axis=1), jnp.concatenate([high, shift_l[c]], axis=0)
        )

    for c in columns:
        half = 0.5 * scale[c]
        for a in range(count):
            for b in range(count):
                value = (prod[c, at(a), at(b)] + prod[c, at(b), at(a)].T) * half
                sq_h[c, at(a), at(b)], sq_l[c, at(a), at(b)] = split(value)

    first = pl.multiple_of(place[0] * rows, rows)
    part_eye = eye(rows, width, first)
    own = pl.ds(first, rows)
    sq_s = [(sq_h[c], sq_l[c]) for c in columns]
    if rows % PACKED:
        x0 = [whole[c, own, :] for c in columns]
    else:
        x0 = [shift_h[c, own, :].astype(F32) + 0.5 * shift_l[c, own, :].astype(F32) for c in columns]
    x0 = [x0[c] * jnp.sqrt(scale[c]) for c in columns]
    x1 = [1.5 * x0[c] - 0.5 * dot3(split(x0[c]), sq_s[c]) for c in columns]
    y1 = [1.5 * x1[c] - 0.5 * dot3(split(x1[c]), sq_s[c]) for c in columns]
    y2 = [1.5 * y1[c] - 0.5 * dot3(split(y1[c]), sq_s[c]) for c in columns]
    for c in columns:
        y3 = dot3(split(y2[c]), sq_s[c])
        out[c] = 0.5 * (part_eye - (1.5 * x1[c] - 0.5 * y3))


def call(neighbour_mask, fermi_level, place, m_left, factors, m_right, h_left, hamiltonian_band, h_right, rep_size):
    cols, count, block, _ = hamiltonian_band.shape
    reach = (count - 1) // 2
    width = count * block
    rows = width // rep_size
    depth = factors.shape[1]
    window = (cols + 2 * reach) * block
    smem = pl.BlockSpec(memory_space=pltpu.SMEM)
    vmem = pl.BlockSpec(memory_space=pltpu.VMEM)
    return pl.pallas_call(
        functools.partial(kernel, cols, reach, rep_size),
        out_shape=jax.ShapeDtypeStruct((cols, rows, width), F32),
        in_specs=[smem] * 3 + [vmem] * 6,
        out_specs=vmem,
        scratch_shapes=[
            pltpu.VMEM((window, window), F32),
            pltpu.VMEM((window, window), BF16),
            pltpu.VMEM((window, window), BF16),
            pltpu.VMEM((cols, depth, width), BF16),
            pltpu.VMEM((cols, depth, width), BF16),
            pltpu.VMEM((cols, width, depth), BF16),
            pltpu.VMEM((cols, width, depth), BF16),
            pltpu.VMEM((cols, width, width), F32),
            pltpu.VMEM((cols, width, width), BF16),
            pltpu.VMEM((cols, width, width), BF16),
            pltpu.VMEM((cols, width, width), BF16),
            pltpu.VMEM((cols, width, width), BF16),
            pltpu.VMEM((cols, width, depth), BF16),
            pltpu.VMEM((cols, width, depth), BF16),
            pltpu.VMEM((cols, width, width) if rows % PACKED else (1, 8, 128), F32),
        ],
        compiler_params=pltpu.CompilerParams(vmem_limit_bytes=48 * 2**20),
    )(neighbour_mask, fermi_level, place, m_left, factors, m_right, h_left, hamiltonian_band, h_right)


def extended(value, reach):
    count = lax.axis_size("cols")
    forward = [(i, (i + 1) % count) for i in range(count)]
    backward = [(target, source) for source, target in forward]
    size = value.shape[0]
    low = lax.ppermute(lax.slice_in_dim(value, size - reach, size, axis=0), "cols", forward)
    high = lax.ppermute(lax.slice_in_dim(value, 0, reach, axis=0), "cols", backward)
    return low, high


def on_device(hamiltonian_band, margin_factors, neighbour_mask, fermi_level):
    cols, count, block, _ = hamiltonian_band.shape
    reach = (count - 1) // 2
    rep_size = lax.axis_size("rep")
    h_left, h_right = extended(hamiltonian_band, reach)
    factors = lax.all_gather(margin_factors, "rep", axis=1, tiled=True)
    m_left, m_right = extended(factors, reach)
    place = lax.axis_index("rep").astype(jnp.int32).reshape(1)
    return call(neighbour_mask, fermi_level, place, m_left, factors, m_right, h_left, hamiltonian_band, h_right, rep_size)


def solution(mesh):
    in_specs = (P("cols", None, None, None), P("cols", "rep", None), P("cols", None), P())
    out_specs = P("cols", "rep", None)
    return jax.shard_map(
        on_device, mesh=mesh, in_specs=in_specs, out_specs=out_specs, check_vma=False
    )
```

```python
import functools

import jax
import jax.numpy as jnp
from jax import lax
from jax.experimental import pallas as pl
from jax.experimental.pallas import tpu as pltpu
from jax.sharding import PartitionSpec as P

F32 = jnp.float32
BF16 = jnp.bfloat16
PACKED = 16
TILE = 8


def split(value):
    high = value.astype(BF16)
    return high, (value - high.astype(F32)).astype(BF16)


def dot(left, right):
    return jnp.dot(left, right, preferred_element_type=F32)


def dot3(left, right):
    (left_high, left_low), (right_high, right_low) = left, right
    return dot(
        jnp.concatenate([left_high, left_low, left_high], axis=1),
        jnp.concatenate([right_high, right_high, right_low], axis=0),
    )


def total(value):
    return jnp.sum(jnp.sum(value, axis=0, keepdims=True), axis=1, keepdims=True)


def eye(rows, columns, first=0):
    row = lax.broadcasted_iota(jnp.int32, (rows, columns), 0) + first
    column = lax.broadcasted_iota(jnp.int32, (rows, columns), 1)
    return jnp.where(row == column, 1.0, 0.0).astype(F32)


def upper(block):
    row = lax.broadcasted_iota(jnp.int32, (block, block), 0)
    return row <= lax.broadcasted_iota(jnp.int32, (block, block), 1)


def crossing(reach):
    return [(i, j) for j in range(reach) for i in range(reach) if reach + j - i <= reach]


def edge_kernel(reach, even, band, far, near, kept):
    block = band.shape[2]
    cross = crossing(reach)
    first = 0.5 * (band[0, reach] + band[0, reach].T)
    second = 0.5 * (band[1, reach] + band[1, reach].T)
    below = 0.5 * (band[0, reach + 1] + band[1, reach - 1].T)
    mixed = jnp.where(upper(block), first, second)
    diagonal = jnp.sum(second * eye(block, block), axis=0, keepdims=True)
    for out in (far, near):
        out[0:block] = mixed
        out[block : 2 * block] = below
        out[(2 + len(cross)) * block :] = jnp.broadcast_to(diagonal, (TILE, block))
    kept[0] = first
    kept[1] = below
    kept[2] = second
    is_even = even[0] == 1
    for index, (i, j) in enumerate(cross):
        to_left = band[j, i - j]
        to_right = band[i, 2 * reach + j - i]
        here = slice((2 + index) * block, (3 + index) * block)
        far[here] = jnp.where(is_even, to_left, to_right)
        near[here] = jnp.where(is_even, to_right, to_left)
        kept[3 + index] = to_left
        kept[3 + len(cross) + index] = to_right


def root_kernel(cols, reach, rep_size, even, mask, *refs):
    groups = refs[:rep_size]
    nears = refs[rep_size : 2 * rep_size]
    y_h, y_l, yt_h, yt_l, poly, unit = refs[2 * rep_size :]
    piece, block = groups[0].shape[1:]
    count = 2 * reach + 1
    window = cols + 2 * reach
    width = count * block
    columns = range(cols)
    is_even = even[0] == 1

    def margin(w):
        parts = []
        for group, near in zip(groups, nears):
            if reach <= w < reach + cols:
                parts.append(group[w - reach])
            elif w < reach:
                parts.append(jnp.where(is_even, group[cols + w], near[w]))
            else:
                parts.append(jnp.where(is_even, near[w - reach - cols], group[w - reach]))
        return jnp.concatenate(parts, axis=0)

    def at(index):
        return slice(index * block, (index + 1) * block)

    keep = [[mask[c, a].astype(F32) for a in range(count)] for c in columns]
    trace = [jnp.zeros((1, 1), F32) for _ in columns]
    for w in range(window):
        x = margin(w)
        xt = x.T
        x_sq = total(x * x)
        for c in columns:
            a = w - c
            if 0 <= a < count:
                m = keep[c][a]
                y_h[c, :, at(a)], y_l[c, :, at(a)] = split(x * m)
                yt_h[c, at(a), :], yt_l[c, at(a), :] = split(xt * m)
                trace[c] = trace[c] + x_sq * m

    depth = piece * rep_size
    small_eye = eye(depth, depth)
    gram = [dot3((y_h[c], y_l[c]), (yt_h[c], yt_l[c])) for c in columns]
    coef = []
    kappa = []
    for c in columns:
        sum_sq = width + 2.0 * trace[c] + total(gram[c] * gram[c])
        s0 = 1.0 / (2.0 * jnp.sqrt(sum_sq / width))
        t0 = 1.5 - 0.5 * s0
        u0 = 1.5 - 0.5 * t0 * t0 * s0
        u1 = 0.5 * t0 * (t0 - s0)
        u2 = 0.5 * (0.25 * s0 - t0)
        u3 = 0.125
        root = jnp.sqrt(s0)
        factor = s0 * root
        e1 = (-t0 * u1 - 0.5 * u0) * factor
        e2 = (-t0 * u2 + 0.5 * u1) * factor
        e3 = (-t0 * u3 + 0.5 * u2) * factor
        e4 = 0.5 * u3 * factor
        unit[c] = jnp.broadcast_to(t0 * u0 * root, unit.shape[1:])
        coef.append((e1, e2, e3, e4))
        kappa.append(gram[c] * s0)
    kappa_s = [split(kappa[c]) for c in columns]
    square = [dot3(kappa_s[c], kappa_s[c]) for c in columns]
    cube = [dot3(kappa_s[c], split(square[c])) for c in columns]
    for c in columns:
        e1, e2, e3, e4 = coef[c]
        poly[c] = e1 * small_eye + e2 * kappa[c] + e3 * square[c] + e4 * cube[c]


def density_kernel(
    cols, reach, rep_size,
    even, mask, fermi, place,
    y_h, y_l, yt_h, yt_l, poly, unit, kept, far, near,
    out,
    ham, ham_h, ham_l, prod, shift_h, shift_l, sq_h, sq_l, side_h, side_l, whole,
):
    depth, width = y_h.shape[1:]
    count = 2 * reach + 1
    block = width // count
    window = cols + 2 * reach
    rows = width // rep_size
    columns = range(cols)
    cross = crossing(reach)
    is_even = even[0] == 1

    def at(index):
        return slice(index * block, (index + 1) * block)

    keep = [[mask[c, a].astype(F32) for a in range(count)] for c in columns]

    half = {}
    for side, base in ((0, 0), (1, reach + cols)):
        def read(index):
            if side == 0:
                return jnp.where(is_even, far[at(index)], near[at(index)])
            return jnp.where(is_even, near[at(index)], far[at(index)])

        end = slice((2 + len(cross)) * block, (2 + len(cross)) * block + 1)
        diagonal = jnp.where(is_even, far[end], near[end]) if side == 0 else jnp.where(is_even, near[end], far[end])
        mixed = read(0)
        one = jnp.where(upper(block), mixed, 0.0)
        two = mixed - one
        half[base, base] = one + two_sided(one, block)
        half[base + 1, base + 1] = two + two.T + diagonal * eye(block, block)
        half[base + 1, base] = read(1)
        for index, (i, j) in enumerate(cross):
            raw = read(2 + index)
            if side == 0:
                half[reach + j, i] = 0.5 * (raw + kept[3 + index].T)
            else:
                half[reach + cols + j, reach + i] = 0.5 * (kept[3 + len(cross) + index] + raw.T)
    half[reach, reach] = kept[0]
    half[reach + 1, reach] = kept[1]
    half[reach + 1, reach + 1] = kept[2]
    for a in range(window):
        for b in range(a + 1):
            if a - b <= reach:
                value = half[a, b]
                ham[at(a), at(b)] = value
                ham_h[at(a), at(b)], ham_l[at(a), at(b)] = split(value)
                if a != b:
                    value = value.T
                    ham[at(b), at(a)] = value
                    ham_h[at(b), at(a)], ham_l[at(b), at(a)] = split(value)
            else:
                none = jnp.zeros((block, block), BF16)
                for i, j in ((a, b), (b, a)):
                    ham_h[at(i), at(j)] = none
                    ham_l[at(i), at(j)] = none

    for c in columns:
        for begin, end in ((0, reach), (reach, reach + 1), (reach + 1, count)):
            low, high = max(0, begin - reach), min(count, end + reach)
            here = slice((c + begin) * block, (c + end) * block), slice((c + low) * block, (c + high) * block)
            inner = slice(low * block, high * block)
            side = dot3((ham_h[here], ham_l[here]), (yt_h[c, inner, :], yt_l[c, inner, :]))
            for a in range(begin, end):
                side_h[c, at(a), :], side_l[c, at(a), :] = split(side[at(a - begin)] * keep[c][a])
    core = [dot3((y_h[c], y_l[c]), (side_h[c], side_l[c])) for c in columns]

    poly_s = [split(poly[c]) for c in columns]
    core = [dot3(poly_s[c], split(core[c])) for c in columns]
    core = [dot3(split(core[c]), poly_s[c]) for c in columns]
    factor = []
    for c in columns:
        left = tuple(
            jnp.concatenate(pair, axis=1) for pair in ((side_h[c], yt_h[c]), (side_l[c], yt_l[c]))
        )
        right = split(jnp.concatenate([unit[c, 0:1, 0:1] * poly[c], 0.5 * core[c]], axis=0))
        factor.append(split(dot3(left, right)))
    for c in columns:
        prod[c] = dot3(factor[c], (y_h[c], y_l[c]))

    level = fermi[0] * eye(block, block)
    scale = []
    for c in columns:
        z0 = unit[c, 0:1, 0:1]
        z0_sq = z0 * z0
        sum_sq = jnp.zeros((block, block), F32)
        for a in range(count):
            for b in range(count):
                value = prod[c, at(a), at(b)] + prod[c, at(b), at(a)].T
                if abs(a - b) <= reach:
                    value = value + ham[at(c + a), at(c + b)] * (z0_sq * (keep[c][a] * keep[c][b]))
                if a == b:
                    value = value - level
                sum_sq = sum_sq + value * value
                if rows % PACKED:
                    whole[c, at(a), at(b)] = value
                high = value.astype(BF16)
                shift_h[c, at(a), at(b)] = high
                shift_l[c, at(a), at(b)] = (2.0 * (value - high.astype(F32))).astype(BF16)
        scale.append(1.0 / (4.0 * (total(sum_sq) / width + 1e-05)))

    for c in columns:
        high = shift_h[c]
        prod[c] = dot(
            jnp.concatenate([high, high], axis=1), jnp.concatenate([high, shift_l[c]], axis=0)
        )

    for c in columns:
        factor_c = 0.5 * scale[c]
        for a in range(count):
            for b in range(count):
                value = (prod[c, at(a), at(b)] + prod[c, at(b), at(a)].T) * factor_c
                sq_h[c, at(a), at(b)], sq_l[c, at(a), at(b)] = split(value)

    first = pl.multiple_of(place[0] * rows, rows)
    part_eye = eye(rows, width, first)
    own = pl.ds(first, rows)
    sq_s = [(sq_h[c], sq_l[c]) for c in columns]
    if rows % PACKED:
        x0 = [whole[c, own, :] for c in columns]
    else:
        x0 = [shift_h[c, own, :].astype(F32) + 0.5 * shift_l[c, own, :].astype(F32) for c in columns]
    x0 = [x0[c] * jnp.sqrt(scale[c]) for c in columns]
    x1 = [1.5 * x0[c] - 0.5 * dot3(split(x0[c]), sq_s[c]) for c in columns]
    y1 = [1.5 * x1[c] - 0.5 * dot3(split(x1[c]), sq_s[c]) for c in columns]
    y2 = [1.5 * y1[c] - 0.5 * dot3(split(y1[c]), sq_s[c]) for c in columns]
    for c in columns:
        y3 = dot3(split(y2[c]), sq_s[c])
        out[c] = 0.5 * (part_eye - (1.5 * x1[c] - 0.5 * y3))


def two_sided(one, block):
    return jnp.where(upper(block), 0.0, one.T)


def shaped(*shape, dtype=F32):
    return jax.ShapeDtypeStruct(shape, dtype)


SMEM = pl.BlockSpec(memory_space=pltpu.SMEM)
VMEM = pl.BlockSpec(memory_space=pltpu.VMEM)


def edges(even, band):
    cols, count, block, _ = band.shape
    reach = (count - 1) // 2
    cross = len(crossing(reach))
    height = (2 + cross) * block + TILE
    return pl.pallas_call(
        functools.partial(edge_kernel, reach),
        out_shape=[shaped(height, block), shaped(height, block), shaped(3 + 2 * cross, block, block)],
        in_specs=[SMEM, VMEM],
        out_specs=[VMEM] * 3,
        compiler_params=pltpu.CompilerParams(vmem_limit_bytes=8 * 2**20),
        cost_estimate=pl.CostEstimate(flops=0, bytes_accessed=4 * 2**20, transcendentals=0),
    )(even, band)


def inverse_root(even, mask, groups, nears, cols):
    rep_size = len(groups)
    piece, block = groups[0].shape[1:]
    reach = groups[0].shape[0] - cols
    depth = piece * rep_size
    width = (2 * reach + 1) * block
    return pl.pallas_call(
        functools.partial(root_kernel, cols, reach, rep_size),
        out_shape=[
            shaped(cols, depth, width, dtype=BF16),
            shaped(cols, depth, width, dtype=BF16),
            shaped(cols, width, depth, dtype=BF16),
            shaped(cols, width, depth, dtype=BF16),
            shaped(cols, depth, depth),
            shaped(cols, TILE, block),
        ],
        in_specs=[SMEM] * 2 + [VMEM] * (2 * rep_size),
        out_specs=[VMEM] * 6,
        compiler_params=pltpu.CompilerParams(vmem_limit_bytes=16 * 2**20),
        cost_estimate=pl.CostEstimate(flops=2**30, bytes_accessed=4 * 2**20, transcendentals=0),
    )(even, mask, *groups, *nears)


def density(even, mask, fermi, place, root, kept, far, near, reach, rep_size):
    cols, depth, width = root[0].shape
    rows = width // rep_size
    block = width // (2 * reach + 1)
    window = (cols + 2 * reach) * block
    return pl.pallas_call(
        functools.partial(density_kernel, cols, reach, rep_size),
        out_shape=shaped(cols, rows, width),
        in_specs=[SMEM] * 4 + [VMEM] * 9,
        out_specs=VMEM,
        scratch_shapes=[
            pltpu.VMEM((window, window), F32),
            pltpu.VMEM((window, window), BF16),
            pltpu.VMEM((window, window), BF16),
            pltpu.VMEM((cols, width, width), F32),
            pltpu.VMEM((cols, width, width), BF16),
            pltpu.VMEM((cols, width, width), BF16),
            pltpu.VMEM((cols, width, width), BF16),
            pltpu.VMEM((cols, width, width), BF16),
            pltpu.VMEM((cols, width, depth), BF16),
            pltpu.VMEM((cols, width, depth), BF16),
            pltpu.VMEM((cols, width, width) if rows % PACKED else (1, TILE, block), F32),
        ],
        compiler_params=pltpu.CompilerParams(vmem_limit_bytes=36 * 2**20),
        cost_estimate=pl.CostEstimate(flops=2**34, bytes_accessed=8 * 2**20, transcendentals=0),
    )(even, mask, fermi, place, *root, kept, far, near)


def near_swap(value):
    return lax.ppermute(value, "cols", [(i, i ^ 1) for i in range(lax.axis_size("cols"))])


def far_swap(value):
    count = lax.axis_size("cols")
    return lax.ppermute(value, "cols", [(i, (((i + 1) ^ 1) - 1) % count) for i in range(count)])


def rep_swap(value, step):
    return lax.ppermute(value, "rep", [(i, i ^ step) for i in range(lax.axis_size("rep"))])


def on_device(hamiltonian_band, margin_factors, neighbour_mask, fermi_level):
    cols, count, _, _ = hamiltonian_band.shape
    reach = (count - 1) // 2
    rep_size = lax.axis_size("rep")
    even = 1 - (lax.axis_index("cols").astype(jnp.int32) % 2).reshape(1)
    place = lax.axis_index("rep").astype(jnp.int32).reshape(1)
    margin_far = far_swap(margin_factors)
    margin_near = near_swap(margin_factors)
    to_far, to_near, kept = edges(even, hamiltonian_band)
    far, near = far_swap(to_far), near_swap(to_near)
    margin_far, _ = lax.optimization_barrier((margin_far, kept))
    group = jnp.concatenate([margin_factors, margin_far], axis=0)
    groups = [group] + [rep_swap(group, step) for step in range(1, rep_size)]
    nears = [margin_near] + [near_swap(value) for value in groups[1:]]
    root = inverse_root(even, neighbour_mask, groups, nears, cols)
    return density(even, neighbour_mask, fermi_level, place, root, kept, far, near, reach, rep_size)


def solution(mesh):
    in_specs = (P("cols", None, None, None), P("cols", "rep", None), P("cols", None), P())
    out_specs = P("cols", "rep", None)
    return jax.shard_map(
        on_device, mesh=mesh, in_specs=in_specs, out_specs=out_specs, check_vma=False
    )
```

```python
import functools

import jax
import jax.numpy as jnp
from jax import lax
from jax.experimental import pallas as pl
from jax.experimental.pallas import tpu as pltpu
from jax.sharding import PartitionSpec as P

F32 = jnp.float32
BF16 = jnp.bfloat16
PACKED = 16
STEP = 256
TILE = 8


def split(value):
    high = value.astype(BF16)
    return high, (value - high.astype(F32)).astype(BF16)


def dot(left, right):
    return jnp.dot(left, right, preferred_element_type=F32)


def dot3(left, right):
    (left_high, left_low), (right_high, right_low) = left, right
    return dot(
        jnp.concatenate([left_high, left_low, left_high], axis=1),
        jnp.concatenate([right_high, right_high, right_low], axis=0),
    )


def total(value):
    return jnp.sum(jnp.sum(value, axis=0, keepdims=True), axis=1, keepdims=True)


def eye(rows, columns, first=0):
    row = lax.broadcasted_iota(jnp.int32, (rows, columns), 0) + first
    column = lax.broadcasted_iota(jnp.int32, (rows, columns), 1)
    return jnp.where(row == column, 1.0, 0.0).astype(F32)


def upper(block):
    row = lax.broadcasted_iota(jnp.int32, (block, block), 0)
    return row <= lax.broadcasted_iota(jnp.int32, (block, block), 1)


def crossing(reach):
    return [(i, j) for j in range(reach) for i in range(reach) if reach + j - i <= reach]


def edge_kernel(reach, even, band, own, far, near, kept):
    block = band.shape[2]
    cross = crossing(reach)
    first = 0.5 * (band[0, reach] + band[0, reach].T)
    second = 0.5 * (band[1, reach] + band[1, reach].T)
    below = 0.5 * (band[0, reach + 1] + band[1, reach - 1].T)
    mixed = jnp.where(upper(block), first, second)
    diagonal = jnp.sum(second * eye(block, block), axis=0, keepdims=True)
    for out in (far, near):
        out[0:block] = mixed
        out[block : 2 * block] = below
        end = (2 + len(cross)) * block
        out[end : end + TILE] = jnp.broadcast_to(diagonal, (TILE, block))
    cols, piece, _ = own.shape
    for c in range(cols):
        begin = near.shape[0] + (c - cols) * piece
        near[begin : begin + piece] = own[c]
    kept[0] = first
    kept[1] = below
    kept[2] = second
    is_even = even[0] == 1
    for index, (i, j) in enumerate(cross):
        to_left = band[j, i - j]
        to_right = band[i, 2 * reach + j - i]
        here = slice((2 + index) * block, (3 + index) * block)
        far[here] = jnp.where(is_even, to_left, to_right)
        near[here] = jnp.where(is_even, to_right, to_left)
        kept[3 + index] = to_left
        kept[3 + len(cross) + index] = to_right


def root_kernel(cols, reach, rep_size, even, mask, *refs):
    owns = refs[:rep_size]
    fars = refs[rep_size : 2 * rep_size]
    nears = refs[2 * rep_size : 3 * rep_size]
    y_h, y_l, yt_h, yt_l, p_h, p_l, pt_h, pt_l, unit = refs[3 * rep_size :]
    piece, block = owns[0].shape[1:]
    count = 2 * reach + 1
    window = cols + 2 * reach
    width = count * block
    columns = range(cols)
    is_even = even[0] == 1

    def margin(w):
        parts = []
        for own, far, near in zip(owns, fars, nears):
            if reach <= w < reach + cols:
                parts.append(own[w - reach])
                continue
            index = w if w < reach else w - reach - cols
            from_far = far[far.shape[0] - cols + index]
            if len(near.shape) == 2:
                begin = near.shape[0] + (index - cols) * piece
                from_near = near[begin : begin + piece]
            else:
                from_near = near[index]
            pair = from_far, from_near
            parts.append(jnp.where(is_even, *(pair if w < reach else pair[::-1])))
        return jnp.concatenate(parts, axis=0)

    def at(index):
        return slice(index * block, (index + 1) * block)

    keep = [[mask[c, a].astype(F32) for a in range(count)] for c in columns]
    for w in range(window):
        x = margin(w)
        xt = x.T
        for c in columns:
            a = w - c
            if 0 <= a < count:
                m = keep[c][a]
                y_h[c, :, at(a)], y_l[c, :, at(a)] = split(x * m)
                yt_h[c, at(a), :], yt_l[c, at(a), :] = split(xt * m)

    depth = piece * rep_size
    small_eye = eye(depth, depth)
    gram = [dot3((y_h[c], y_l[c]), (yt_h[c], yt_l[c])) for c in columns]
    gram_s = [split(gram[c]) for c in columns]
    square = [dot3(gram_s[c], gram_s[c]) for c in columns]
    cube = [dot3(gram_s[c], split(square[c])) for c in columns]
    poly = []
    for c in columns:
        sum_sq = width + total(gram[c] * (gram[c] + 2.0 * small_eye))
        s0 = 1.0 / (2.0 * jnp.sqrt(sum_sq / width))
        t0 = 1.5 - 0.5 * s0
        u0 = 1.5 - 0.5 * t0 * t0 * s0
        u1 = 0.5 * t0 * (t0 - s0)
        u2 = 0.5 * (0.25 * s0 - t0)
        u3 = 0.125
        root = jnp.sqrt(s0)
        e1 = (-t0 * u1 - 0.5 * u0) * (root * s0)
        e2 = (-t0 * u2 + 0.5 * u1) * (root * s0 * s0)
        e3 = (-t0 * u3 + 0.5 * u2) * (root * s0 * s0 * s0)
        e4 = 0.5 * u3 * (root * s0 * s0 * s0 * s0)
        unit[c] = jnp.broadcast_to(t0 * u0 * root, unit.shape[1:])
        poly.append(split(e1 * small_eye + e2 * gram[c] + e3 * square[c] + e4 * cube[c]))
    for c in columns:
        p = dot3(poly[c], (y_h[c], y_l[c]))
        p_h[c], p_l[c] = split(p)
        for a in range(count):
            pt_h[c, at(a), :], pt_l[c, at(a), :] = split(p[:, at(a)].T)


def density_kernel(
    cols, reach, rep_size,
    even, mask, fermi, place,
    y_h, y_l, yt_h, yt_l, p_h, p_l, pt_h, pt_l, unit, kept, far, near,
    target,
    ham, ham_h, ham_l, whole, out, sent, *scratch,
):
    prod, shift_h, shift_l, sq_h, sq_l, cross_side, side_h, side_l, tail = (
        scratch[begin : begin + cols] for begin in range(0, 9 * cols, cols)
    )
    depth, width = y_h.shape[1:]
    count = 2 * reach + 1
    block = width // count
    window = cols + 2 * reach
    rows = width // rep_size
    columns = range(cols)
    cross = crossing(reach)
    is_even = even[0] == 1

    def at(index):
        return slice(index * block, (index + 1) * block)

    keep = [[mask[c, a].astype(F32) for a in range(count)] for c in columns]

    half = {}
    for side, base in ((0, 0), (1, reach + cols)):
        def read(index):
            if side == 0:
                return jnp.where(is_even, far[at(index)], near[at(index)])
            return jnp.where(is_even, near[at(index)], far[at(index)])

        end = slice((2 + len(cross)) * block, (2 + len(cross)) * block + 1)
        diagonal = jnp.where(is_even, far[end], near[end]) if side == 0 else jnp.where(is_even, near[end], far[end])
        mixed = read(0)
        one = jnp.where(upper(block), mixed, 0.0)
        two = mixed - one
        half[base, base] = one + two_sided(one, block)
        half[base + 1, base + 1] = two + two.T + diagonal * eye(block, block)
        half[base + 1, base] = read(1)
        for index, (i, j) in enumerate(cross):
            raw = read(2 + index)
            if side == 0:
                half[reach + j, i] = 0.5 * (raw + kept[3 + index].T)
            else:
                half[reach + cols + j, reach + i] = 0.5 * (kept[3 + len(cross) + index] + raw.T)
    half[reach, reach] = kept[0]
    half[reach + 1, reach] = kept[1]
    half[reach + 1, reach + 1] = kept[2]
    for a in range(window):
        for b in range(a + 1):
            if a - b <= reach:
                value = half[a, b]
                ham[at(a), at(b)] = value
                ham_h[at(a), at(b)], ham_l[at(a), at(b)] = split(value)
                if a != b:
                    value = value.T
                    ham[at(b), at(a)] = value
                    ham_h[at(b), at(a)], ham_l[at(b), at(a)] = split(value)
            else:
                none = jnp.zeros((block, block), BF16)
                for i, j in ((a, b), (b, a)):
                    ham_h[at(i), at(j)] = none
                    ham_l[at(i), at(j)] = none

    for c in columns:
        for begin, end in ((0, reach), (reach, reach + 1), (reach + 1, count)):
            low, high = max(0, begin - reach), min(count, end + reach)
            here = slice((c + begin) * block, (c + end) * block), slice((c + low) * block, (c + high) * block)
            inner = slice(low * block, high * block)
            part = dot3((ham_h[here], ham_l[here]), (pt_h[c, inner, :], pt_l[c, inner, :]))
            for a in range(begin, end):
                value = part[at(a - begin)] * keep[c][a]
                cross_side[c][at(a), :] = value
                side_h[c][at(a), :], side_l[c][at(a), :] = split(value)
    core = [split(dot3((p_h[c], p_l[c]), (side_h[c][...], side_l[c][...]))) for c in columns]

    factor = []
    for c in columns:
        value = unit[c, 0:1, 0:1] * cross_side[c][...] + 0.5 * dot3((yt_h[c], yt_l[c]), core[c])
        factor.append(split(value))
    for c in columns:
        prod[c][...] = dot3(factor[c], (y_h[c], y_l[c]))

    level = fermi[0] * eye(block, block)
    scale = []
    for c in columns:
        z0 = unit[c, 0:1, 0:1]
        z0_sq = z0 * z0
        sum_sq = jnp.zeros((block, block), F32)
        for a in range(count):
            for b in range(a + 1):
                value = prod[c][at(a), at(b)] + prod[c][at(b), at(a)].T
                if a - b <= reach:
                    value = value + ham[at(c + a), at(c + b)] * (z0_sq * (keep[c][a] * keep[c][b]))
                if a == b:
                    value = value - level
                sum_sq = sum_sq + value * value * (1.0 if a == b else 2.0)
                for i, j in ((a, b), (b, a))[: 1 + (a != b)]:
                    if (i, j) != (a, b):
                        value = value.T
                    if rows % PACKED:
                        whole[c, at(i), at(j)] = value
                    high = value.astype(BF16)
                    shift_h[c][at(i), at(j)] = high
                    shift_l[c][at(i), at(j)] = (2.0 * (value - high.astype(F32))).astype(BF16)
        scale.append(1.0 / (4.0 * (total(sum_sq) / width + 1e-05)))

    edge = width - block
    for c in columns:
        high, low = shift_h[c][...], shift_l[c][...]
        prod[c][:, :edge] = dot(
            jnp.concatenate([high, high], axis=1),
            jnp.concatenate([high[:, :edge], low[:, :edge]], axis=0),
        )
        tail[c][...] = dot(
            jnp.concatenate([high[edge:], low[edge:]], axis=1), jnp.concatenate([high, high], axis=0)
        )

    first = pl.multiple_of(place[0] * rows, rows)
    part_eye = eye(rows, width, first)
    own = pl.ds(first, rows)

    def scaled(c):
        factor_c = 0.5 * scale[c]
        for a in range(count):
            for b in range(a + 1):
                if a < count - 1:
                    value = prod[c][at(a), at(b)] + prod[c][at(b), at(a)].T
                elif b < a:
                    value = prod[c][at(a), at(b)] + tail[c][:, at(b)]
                else:
                    value = tail[c][:, at(b)]
                    value = value + value.T
                value = value * factor_c
                sq_h[c][at(a), at(b)], sq_l[c][at(a), at(b)] = split(value)
                if a != b:
                    sq_h[c][at(b), at(a)], sq_l[c][at(b), at(a)] = split(value.T)

    if rows % PACKED:
        x0 = [whole[c, own, :] for c in columns]
    else:
        x0 = [shift_h[c][own, :].astype(F32) + 0.5 * shift_l[c][own, :].astype(F32) for c in columns]
    x0 = [x0[c] * jnp.sqrt(scale[c]) for c in columns]
    sq_s, x1 = [], []
    for c in columns:
        scaled(c)
        sq_s.append((sq_h[c][...], sq_l[c][...]))
        x1.append(1.5 * x0[c] - 0.5 * dot3(split(x0[c]), sq_s[c]))
    y1 = [1.5 * x1[c] - 0.5 * dot3(split(x1[c]), sq_s[c]) for c in columns]
    y2 = [1.5 * y1[c] - 0.5 * dot3(split(y1[c]), sq_s[c]) for c in columns]
    copies = []
    for c in columns:
        left = split(y2[c])
        for index, begin in enumerate(range(0, width, STEP)):
            here = slice(begin, min(begin + STEP, width))
            y3 = dot3(left, (sq_h[c][:, here], sq_l[c][:, here]))
            out[c, :, here] = 0.5 * (part_eye[:, here] - (1.5 * x1[c][:, here] - 0.5 * y3))
            copies.append(
                pltpu.make_async_copy(out.at[c, :, here], target.at[c, :, here], sent.at[c, index])
            )
            copies[-1].start()
    for copy in copies:
        copy.wait()


def two_sided(one, block):
    return jnp.where(upper(block), 0.0, one.T)


def shaped(*shape, dtype=F32):
    return jax.ShapeDtypeStruct(shape, dtype)


SMEM = pl.BlockSpec(memory_space=pltpu.SMEM)
VMEM = pl.BlockSpec(memory_space=pltpu.VMEM)


def edges(even, band, own):
    cols, count, block, _ = band.shape
    reach = (count - 1) // 2
    cross = len(crossing(reach))
    height = (2 + cross) * block + TILE
    return pl.pallas_call(
        functools.partial(edge_kernel, reach),
        out_shape=[shaped(height, block), shaped(height + own.shape[0] * own.shape[1], block), shaped(3 + 2 * cross, block, block)],
        in_specs=[SMEM, VMEM, VMEM],
        out_specs=[VMEM] * 3,
        compiler_params=pltpu.CompilerParams(vmem_limit_bytes=8 * 2**20),
        cost_estimate=pl.CostEstimate(flops=0, bytes_accessed=4 * 2**20, transcendentals=0),
    )(even, band, own)


def inverse_root(even, mask, owns, fars, nears, reach):
    rep_size = len(owns)
    cols, piece, block = owns[0].shape
    depth = piece * rep_size
    width = (2 * reach + 1) * block
    return pl.pallas_call(
        functools.partial(root_kernel, cols, reach, rep_size),
        out_shape=[
            shaped(cols, depth, width, dtype=BF16),
            shaped(cols, depth, width, dtype=BF16),
            shaped(cols, width, depth, dtype=BF16),
            shaped(cols, width, depth, dtype=BF16),
            shaped(cols, depth, width, dtype=BF16),
            shaped(cols, depth, width, dtype=BF16),
            shaped(cols, width, depth, dtype=BF16),
            shaped(cols, width, depth, dtype=BF16),
            shaped(cols, TILE, block),
        ],
        in_specs=[SMEM] * 2 + [VMEM] * (3 * rep_size),
        out_specs=[VMEM] * 9,
        compiler_params=pltpu.CompilerParams(vmem_limit_bytes=16 * 2**20),
        cost_estimate=pl.CostEstimate(flops=2**30, bytes_accessed=4 * 2**20, transcendentals=0),
    )(even, mask, *owns, *fars, *nears)


def density(even, mask, fermi, place, root, kept, far, near, reach, rep_size):
    cols, depth, width = root[0].shape
    rows = width // rep_size
    block = width // (2 * reach + 1)
    window = (cols + 2 * reach) * block
    return pl.pallas_call(
        functools.partial(density_kernel, cols, reach, rep_size),
        out_shape=shaped(cols, rows, width),
        in_specs=[SMEM] * 4 + [VMEM] * 12,
        out_specs=pl.BlockSpec(memory_space=pl.ANY),
        scratch_shapes=[
            pltpu.VMEM((window, window), F32),
            pltpu.VMEM((window, window), BF16),
            pltpu.VMEM((window, window), BF16),
            pltpu.VMEM((cols, width, width) if rows % PACKED else (1, TILE, block), F32),
            pltpu.VMEM((cols, rows, width), F32),
            pltpu.SemaphoreType.DMA((cols, pl.cdiv(width, STEP))),
            *[pltpu.VMEM((width, width), F32)] * cols,
            *[pltpu.VMEM((width, width), BF16)] * (4 * cols),
            *[pltpu.VMEM((width, depth), F32)] * cols,
            *[pltpu.VMEM((width, depth), BF16)] * (2 * cols),
            *[pltpu.VMEM((block, width), F32)] * cols,
        ],
        compiler_params=pltpu.CompilerParams(vmem_limit_bytes=36 * 2**20),
        cost_estimate=pl.CostEstimate(flops=2**34, bytes_accessed=8 * 2**20, transcendentals=0),
    )(even, mask, fermi, place, *root, kept, far, near)


def near_swap(value):
    return lax.ppermute(value, "cols", [(i, i ^ 1) for i in range(lax.axis_size("cols"))])


def far_swap(value):
    count = lax.axis_size("cols")
    return lax.ppermute(value, "cols", [(i, (((i + 1) ^ 1) - 1) % count) for i in range(count)])


def rep_swap(value, step):
    return lax.ppermute(value, "rep", [(i, i ^ step) for i in range(lax.axis_size("rep"))])


def on_device(hamiltonian_band, margin_factors, neighbour_mask, fermi_level):
    cols, count, _, _ = hamiltonian_band.shape
    reach = (count - 1) // 2
    rep_size = lax.axis_size("rep")
    even = 1 - (lax.axis_index("cols").astype(jnp.int32) % 2).reshape(1)
    place = lax.axis_index("rep").astype(jnp.int32).reshape(1)
    margin_far = far_swap(margin_factors)
    to_far, to_near, kept = edges(even, hamiltonian_band, margin_factors)
    margin_far, _ = lax.optimization_barrier((margin_far, kept))
    far = far_swap(to_far)
    near = near_swap(to_near)
    group = jnp.concatenate([margin_factors, margin_far], axis=0)
    groups = [group] + [rep_swap(group, step) for step in range(1, rep_size)]
    owns = [margin_factors] + groups[1:]
    fars = [margin_far] + groups[1:]
    nears = [near] + [near_swap(value) for value in groups[1:]]
    root = inverse_root(even, neighbour_mask, owns, fars, nears, reach)
    return density(even, neighbour_mask, fermi_level, place, root, kept, far, near, reach, rep_size)


def solution(mesh):
    in_specs = (P("cols", None, None, None), P("cols", "rep", None), P("cols", None), P())
    out_specs = P("cols", "rep", None)
    return jax.shard_map(
        on_device, mesh=mesh, in_specs=in_specs, out_specs=out_specs, check_vma=False
    )
```

```python
import functools

import jax
import jax.numpy as jnp
from jax import lax
from jax.experimental import pallas as pl
from jax.experimental.pallas import tpu as pltpu
from jax.sharding import PartitionSpec as P

F32 = jnp.float32
BF16 = jnp.bfloat16
PACKED = 16
STEP = 256
TILE = 8


def split(value):
    high = value.astype(BF16)
    return high, (value - high.astype(F32)).astype(BF16)


def dot(left, right):
    return jnp.dot(left, right, preferred_element_type=F32)


def dot3(left, right):
    (left_high, left_low), (right_high, right_low) = left, right
    return dot(
        jnp.concatenate([left_high, left_low, left_high], axis=1),
        jnp.concatenate([right_high, right_high, right_low], axis=0),
    )


def total(value):
    return jnp.sum(jnp.sum(value, axis=0, keepdims=True), axis=1, keepdims=True)


def eye(rows, columns, first=0):
    row = lax.broadcasted_iota(jnp.int32, (rows, columns), 0) + first
    column = lax.broadcasted_iota(jnp.int32, (rows, columns), 1)
    return jnp.where(row == column, 1.0, 0.0).astype(F32)


def upper(block):
    row = lax.broadcasted_iota(jnp.int32, (block, block), 0)
    return row <= lax.broadcasted_iota(jnp.int32, (block, block), 1)


def crossing(reach):
    return [(i, j) for j in range(reach) for i in range(reach) if reach + j - i <= reach]


def edge_kernel(reach, even, band, own, far, near, kept, group):
    block = band.shape[2]
    cross = crossing(reach)
    first = 0.5 * (band[0, reach] + band[0, reach].T)
    second = 0.5 * (band[1, reach] + band[1, reach].T)
    below = 0.5 * (band[0, reach + 1] + band[1, reach - 1].T)
    mixed = jnp.where(upper(block), first, second)
    diagonal = jnp.sum(second * eye(block, block), axis=0, keepdims=True)
    for out in (far, near):
        out[0:block] = mixed
        out[block : 2 * block] = below
        end = (2 + len(cross)) * block
        out[end : end + TILE] = jnp.broadcast_to(diagonal, (TILE, block))
    cols, piece, _ = own.shape
    for c in range(cols):
        group[c] = own[c]
        begin = near.shape[0] + (c - cols) * piece
        near[begin : begin + piece] = own[c]
    kept[0] = first
    kept[1] = below
    kept[2] = second
    is_even = even[0] == 1
    for index, (i, j) in enumerate(cross):
        to_left = band[j, i - j]
        to_right = band[i, 2 * reach + j - i]
        here = slice((2 + index) * block, (3 + index) * block)
        far[here] = jnp.where(is_even, to_left, to_right)
        near[here] = jnp.where(is_even, to_right, to_left)
        kept[3 + index] = to_left
        kept[3 + len(cross) + index] = to_right


def root_kernel(cols, reach, rep_size, even, mask, *refs):
    owns = refs[:rep_size]
    fars = refs[rep_size : 2 * rep_size]
    nears = refs[2 * rep_size : 3 * rep_size]
    y_h, y_l, yt_h, yt_l, p_h, p_l, pt_h, pt_l, unit = refs[3 * rep_size :]
    piece, block = owns[0].shape[1:]
    count = 2 * reach + 1
    window = cols + 2 * reach
    width = count * block
    columns = range(cols)
    is_even = even[0] == 1

    def margin(w):
        parts = []
        for own, far, near in zip(owns, fars, nears):
            if reach <= w < reach + cols:
                parts.append(own[w - reach])
                continue
            index = w if w < reach else w - reach - cols
            from_far = far[far.shape[0] - cols + index]
            if len(near.shape) == 2:
                begin = near.shape[0] + (index - cols) * piece
                from_near = near[begin : begin + piece]
            else:
                from_near = near[index]
            pair = from_far, from_near
            parts.append(jnp.where(is_even, *(pair if w < reach else pair[::-1])))
        return jnp.concatenate(parts, axis=0)

    def at(index):
        return slice(index * block, (index + 1) * block)

    keep = [[mask[c, a].astype(F32) for a in range(count)] for c in columns]
    for w in range(window):
        x = margin(w)
        xt = x.T
        for c in columns:
            a = w - c
            if 0 <= a < count:
                m = keep[c][a]
                y_h[c, :, at(a)], y_l[c, :, at(a)] = split(x * m)
                yt_h[c, at(a), :], yt_l[c, at(a), :] = split(xt * m)

    depth = piece * rep_size
    small_eye = eye(depth, depth)
    gram = [dot3((y_h[c], y_l[c]), (yt_h[c], yt_l[c])) for c in columns]
    gram_s = [split(gram[c]) for c in columns]
    square = [dot3(gram_s[c], gram_s[c]) for c in columns]
    cube = [dot3(gram_s[c], split(square[c])) for c in columns]
    poly = []
    for c in columns:
        sum_sq = width + total(gram[c] * (gram[c] + 2.0 * small_eye))
        s0 = 1.0 / (2.0 * jnp.sqrt(sum_sq / width))
        t0 = 1.5 - 0.5 * s0
        u0 = 1.5 - 0.5 * t0 * t0 * s0
        u1 = 0.5 * t0 * (t0 - s0)
        u2 = 0.5 * (0.25 * s0 - t0)
        u3 = 0.125
        root = jnp.sqrt(s0)
        e1 = (-t0 * u1 - 0.5 * u0) * (root * s0)
        e2 = (-t0 * u2 + 0.5 * u1) * (root * s0 * s0)
        e3 = (-t0 * u3 + 0.5 * u2) * (root * s0 * s0 * s0)
        e4 = 0.5 * u3 * (root * s0 * s0 * s0 * s0)
        unit[c] = jnp.broadcast_to(t0 * u0 * root, unit.shape[1:])
        poly.append(split(e1 * small_eye + e2 * gram[c] + e3 * square[c] + e4 * cube[c]))
    for c in columns:
        p = dot3(poly[c], (y_h[c], y_l[c]))
        p_h[c], p_l[c] = split(p)
        for a in range(count):
            pt_h[c, at(a), :], pt_l[c, at(a), :] = split(p[:, at(a)].T)


def density_kernel(
    cols, reach, rep_size,
    even, mask, fermi, place,
    y_h, y_l, yt_h, yt_l, p_h, p_l, pt_h, pt_l, unit, kept, far, near,
    target,
    ham, ham_h, ham_l, whole, out, sent, *scratch,
):
    prod, shift_h, shift_l, sq_h, sq_l, cross_side, side_h, side_l, tail = (
        scratch[begin : begin + cols] for begin in range(0, 9 * cols, cols)
    )
    depth, width = y_h.shape[1:]
    count = 2 * reach + 1
    block = width // count
    window = cols + 2 * reach
    rows = width // rep_size
    columns = range(cols)
    cross = crossing(reach)
    is_even = even[0] == 1

    def at(index):
        return slice(index * block, (index + 1) * block)

    keep = [[mask[c, a].astype(F32) for a in range(count)] for c in columns]

    half = {}
    for side, base in ((0, 0), (1, reach + cols)):
        def read(index):
            if side == 0:
                return jnp.where(is_even, far[at(index)], near[at(index)])
            return jnp.where(is_even, near[at(index)], far[at(index)])

        end = slice((2 + len(cross)) * block, (2 + len(cross)) * block + 1)
        diagonal = jnp.where(is_even, far[end], near[end]) if side == 0 else jnp.where(is_even, near[end], far[end])
        mixed = read(0)
        one = jnp.where(upper(block), mixed, 0.0)
        two = mixed - one
        half[base, base] = one + two_sided(one, block)
        half[base + 1, base + 1] = two + two.T + diagonal * eye(block, block)
        half[base + 1, base] = read(1)
        for index, (i, j) in enumerate(cross):
            raw = read(2 + index)
            if side == 0:
                half[reach + j, i] = 0.5 * (raw + kept[3 + index].T)
            else:
                half[reach + cols + j, reach + i] = 0.5 * (kept[3 + len(cross) + index] + raw.T)
    half[reach, reach] = kept[0]
    half[reach + 1, reach] = kept[1]
    half[reach + 1, reach + 1] = kept[2]
    for a in range(window):
        for b in range(a + 1):
            if a - b <= reach:
                value = half[a, b]
                ham[at(a), at(b)] = value
                ham_h[at(a), at(b)], ham_l[at(a), at(b)] = split(value)
                if a != b:
                    value = value.T
                    ham[at(b), at(a)] = value
                    ham_h[at(b), at(a)], ham_l[at(b), at(a)] = split(value)
            else:
                none = jnp.zeros((block, block), BF16)
                for i, j in ((a, b), (b, a)):
                    ham_h[at(i), at(j)] = none
                    ham_l[at(i), at(j)] = none

    for c in columns:
        for begin, end in ((0, reach), (reach, reach + 1), (reach + 1, count)):
            low, high = max(0, begin - reach), min(count, end + reach)
            here = slice((c + begin) * block, (c + end) * block), slice((c + low) * block, (c + high) * block)
            inner = slice(low * block, high * block)
            part = dot3((ham_h[here], ham_l[here]), (pt_h[c, inner, :], pt_l[c, inner, :]))
            for a in range(begin, end):
                value = part[at(a - begin)]
                cross_side[c][at(a), :] = value
                side_h[c][at(a), :], side_l[c][at(a), :] = split(value)
    core = [split(dot3((p_h[c], p_l[c]), (side_h[c][...], side_l[c][...]))) for c in columns]
    for c in columns:
        for a in range(count):
            value = (unit[c, 0:1, 0:1] * keep[c][a]) * cross_side[c][at(a), :] + 0.5 * dot3(
                (yt_h[c, at(a), :], yt_l[c, at(a), :]), core[c]
            )
            side_h[c][at(a), :], side_l[c][at(a), :] = split(value)
    for c in columns:
        prod[c][...] = dot3((side_h[c][...], side_l[c][...]), (y_h[c], y_l[c]))

    level = fermi[0] * eye(block, block)
    scale = []
    for c in columns:
        z0 = unit[c, 0:1, 0:1]
        z0_sq = z0 * z0
        sum_sq = jnp.zeros((block, block), F32)
        for a in range(count):
            for b in range(a + 1):
                value = prod[c][at(a), at(b)] + prod[c][at(b), at(a)].T
                if a - b <= reach:
                    value = value + ham[at(c + a), at(c + b)] * (z0_sq * (keep[c][a] * keep[c][b]))
                if a == b:
                    value = value - level
                sum_sq = sum_sq + value * value * (1.0 if a == b else 2.0)
                for i, j in ((a, b), (b, a))[: 1 + (a != b)]:
                    if (i, j) != (a, b):
                        value = value.T
                    if rows % PACKED:
                        whole[c, at(i), at(j)] = value
                    high = value.astype(BF16)
                    shift_h[c][at(i), at(j)] = high
                    shift_l[c][at(i), at(j)] = (2.0 * (value - high.astype(F32))).astype(BF16)
        scale.append(1.0 / (4.0 * (total(sum_sq) / width + 1e-05)))

    edge = width - block
    first = pl.multiple_of(place[0] * rows, rows)
    part_eye = eye(rows, width, first)
    own = pl.ds(first, rows)
    rows_of = [{} for _ in columns]
    copies = []

    def squared(c):
        high, low = shift_h[c][...], shift_l[c][...]
        prod[c][:, :edge] = dot(
            jnp.concatenate([high, high], axis=1),
            jnp.concatenate([high[:, :edge], low[:, :edge]], axis=0),
        )
        tail[c][...] = dot(
            jnp.concatenate([high[edge:], low[edge:]], axis=1), jnp.concatenate([high, high], axis=0)
        )

    def scaled(c):
        factor_c = 0.5 * scale[c]
        for a in range(count):
            for b in range(a + 1):
                if a < count - 1:
                    value = prod[c][at(a), at(b)] + prod[c][at(b), at(a)].T
                elif b < a:
                    value = prod[c][at(a), at(b)] + tail[c][:, at(b)]
                else:
                    value = tail[c][:, at(b)]
                    value = value + value.T
                value = value * factor_c
                sq_h[c][at(a), at(b)], sq_l[c][at(a), at(b)] = split(value)
                if a != b:
                    sq_h[c][at(b), at(a)], sq_l[c][at(b), at(a)] = split(value.T)

    def step(c, source, target_name):
        value = rows_of[c][source]
        rows_of[c][target_name] = 1.5 * value - 0.5 * dot3(split(value), (sq_h[c][...], sq_l[c][...]))

    def start(c):
        if rows % PACKED:
            value = whole[c, own, :]
        else:
            value = shift_h[c][own, :].astype(F32) + 0.5 * shift_l[c][own, :].astype(F32)
        rows_of[c]["x0"] = value * jnp.sqrt(scale[c])
        step(c, "x0", "x1")

    def finish(c):
        left = split(rows_of[c]["y2"])
        for index, begin in enumerate(range(0, width, STEP)):
            here = slice(begin, min(begin + STEP, width))
            y3 = dot3(left, (sq_h[c][:, here], sq_l[c][:, here]))
            out[c, :, here] = 0.5 * (part_eye[:, here] - (1.5 * rows_of[c]["x1"][:, here] - 0.5 * y3))
            copies.append(
                pltpu.make_async_copy(out.at[c, :, here], target.at[c, :, here], sent.at[c, index])
            )
            copies[-1].start()

    stages = [
        squared,
        scaled,
        start,
        lambda c: step(c, "x1", "y1"),
        lambda c: step(c, "y1", "y2"),
        finish,
    ]
    for index in range(len(stages) + cols - 1):
        for c in columns:
            if 0 <= index - c < len(stages):
                stages[index - c](c)
    for copy in copies:
        copy.wait()


def two_sided(one, block):
    return jnp.where(upper(block), 0.0, one.T)


def shaped(*shape, dtype=F32):
    return jax.ShapeDtypeStruct(shape, dtype)


SMEM = pl.BlockSpec(memory_space=pltpu.SMEM)
VMEM = pl.BlockSpec(memory_space=pltpu.VMEM)


def edges(even, band, own):
    cols, count, block, _ = band.shape
    reach = (count - 1) // 2
    cross = len(crossing(reach))
    height = (2 + cross) * block + TILE
    return pl.pallas_call(
        functools.partial(edge_kernel, reach),
        out_shape=[shaped(height, block), shaped(height + own.shape[0] * own.shape[1], block), shaped(3 + 2 * cross, block, block), shaped(cols, *own.shape[1:])],
        in_specs=[SMEM, VMEM, VMEM],
        out_specs=[VMEM] * 4,
        compiler_params=pltpu.CompilerParams(vmem_limit_bytes=8 * 2**20),
        cost_estimate=pl.CostEstimate(flops=0, bytes_accessed=4 * 2**20, transcendentals=0),
    )(even, band, own)


def inverse_root(even, mask, owns, fars, nears, reach):
    rep_size = len(owns)
    cols, piece, block = owns[0].shape
    depth = piece * rep_size
    width = (2 * reach + 1) * block
    return pl.pallas_call(
        functools.partial(root_kernel, cols, reach, rep_size),
        out_shape=[
            shaped(cols, depth, width, dtype=BF16),
            shaped(cols, depth, width, dtype=BF16),
            shaped(cols, width, depth, dtype=BF16),
            shaped(cols, width, depth, dtype=BF16),
            shaped(cols, depth, width, dtype=BF16),
            shaped(cols, depth, width, dtype=BF16),
            shaped(cols, width, depth, dtype=BF16),
            shaped(cols, width, depth, dtype=BF16),
            shaped(cols, TILE, block),
        ],
        in_specs=[SMEM] * 2 + [VMEM] * (3 * rep_size),
        out_specs=[VMEM] * 9,
        compiler_params=pltpu.CompilerParams(vmem_limit_bytes=16 * 2**20),
        cost_estimate=pl.CostEstimate(flops=2**30, bytes_accessed=4 * 2**20, transcendentals=0),
    )(even, mask, *owns, *fars, *nears)


def density(even, mask, fermi, place, root, kept, far, near, reach, rep_size):
    cols, depth, width = root[0].shape
    rows = width // rep_size
    block = width // (2 * reach + 1)
    window = (cols + 2 * reach) * block
    return pl.pallas_call(
        functools.partial(density_kernel, cols, reach, rep_size),
        out_shape=shaped(cols, rows, width),
        in_specs=[SMEM] * 4 + [VMEM] * 12,
        out_specs=pl.BlockSpec(memory_space=pl.ANY),
        scratch_shapes=[
            pltpu.VMEM((window, window), F32),
            pltpu.VMEM((window, window), BF16),
            pltpu.VMEM((window, window), BF16),
            pltpu.VMEM((cols, width, width) if rows % PACKED else (1, TILE, block), F32),
            pltpu.VMEM((cols, rows, width), F32),
            pltpu.SemaphoreType.DMA((cols, pl.cdiv(width, STEP))),
            *[pltpu.VMEM((width, width), F32)] * cols,
            *[pltpu.VMEM((width, width), BF16)] * (4 * cols),
            *[pltpu.VMEM((width, depth), F32)] * cols,
            *[pltpu.VMEM((width, depth), BF16)] * (2 * cols),
            *[pltpu.VMEM((block, width), F32)] * cols,
        ],
        compiler_params=pltpu.CompilerParams(vmem_limit_bytes=36 * 2**20),
        cost_estimate=pl.CostEstimate(flops=2**34, bytes_accessed=8 * 2**20, transcendentals=0),
    )(even, mask, fermi, place, *root, kept, far, near)


def near_swap(value):
    return lax.ppermute(value, "cols", [(i, i ^ 1) for i in range(lax.axis_size("cols"))])


def far_swap(value):
    count = lax.axis_size("cols")
    return lax.ppermute(value, "cols", [(i, (((i + 1) ^ 1) - 1) % count) for i in range(count)])


def rep_swap(value, step):
    return lax.ppermute(value, "rep", [(i, i ^ step) for i in range(lax.axis_size("rep"))])


def on_device(hamiltonian_band, margin_factors, neighbour_mask, fermi_level):
    cols, count, _, _ = hamiltonian_band.shape
    reach = (count - 1) // 2
    rep_size = lax.axis_size("rep")
    even = 1 - (lax.axis_index("cols").astype(jnp.int32) % 2).reshape(1)
    place = lax.axis_index("rep").astype(jnp.int32).reshape(1)
    margin_far = far_swap(margin_factors)
    to_far, to_near, kept, own = edges(even, hamiltonian_band, margin_factors)
    far = far_swap(to_far)
    near = near_swap(to_near)
    group = jnp.concatenate([own, margin_far], axis=0)
    groups = [group] + [rep_swap(group, step) for step in range(1, rep_size)]
    owns = [own] + groups[1:]
    fars = [margin_far] + groups[1:]
    nears = [near] + [near_swap(value) for value in groups[1:]]
    root = inverse_root(even, neighbour_mask, owns, fars, nears, reach)
    return density(even, neighbour_mask, fermi_level, place, root, kept, far, near, reach, rep_size)


def solution(mesh):
    in_specs = (P("cols", None, None, None), P("cols", "rep", None), P("cols", None), P())
    out_specs = P("cols", "rep", None)
    return jax.shard_map(
        on_device, mesh=mesh, in_specs=in_specs, out_specs=out_specs, check_vma=False
    )
```

```python
import functools

import jax
import jax.numpy as jnp
from jax import lax
from jax.experimental import pallas as pl
from jax.experimental.pallas import tpu as pltpu
from jax.sharding import PartitionSpec as P

F32 = jnp.float32
BF16 = jnp.bfloat16
PACKED = 16
STEP = 256
TILE = 8


def split(value):
    high = value.astype(BF16)
    return high, (value - high.astype(F32)).astype(BF16)


def dot(left, right):
    return jnp.dot(left, right, preferred_element_type=F32)


def dot3(left, right):
    (left_high, left_low), (right_high, right_low) = left, right
    return dot(
        jnp.concatenate([left_high, left_low, left_high], axis=1),
        jnp.concatenate([right_high, right_high, right_low], axis=0),
    )


def total(value):
    return jnp.sum(jnp.sum(value, axis=0, keepdims=True), axis=1, keepdims=True)


def eye(rows, columns, first=0):
    row = lax.broadcasted_iota(jnp.int32, (rows, columns), 0) + first
    column = lax.broadcasted_iota(jnp.int32, (rows, columns), 1)
    return jnp.where(row == column, 1.0, 0.0).astype(F32)


def upper(block):
    row = lax.broadcasted_iota(jnp.int32, (block, block), 0)
    return row <= lax.broadcasted_iota(jnp.int32, (block, block), 1)


def crossing(reach):
    return [(i, j) for j in range(reach) for i in range(reach) if reach + j - i <= reach]


def edge_kernel(reach, even, band, own, far, near, kept, group):
    block = band.shape[2]
    cross = crossing(reach)
    first = 0.5 * (band[0, reach] + band[0, reach].T)
    second = 0.5 * (band[1, reach] + band[1, reach].T)
    below = 0.5 * (band[0, reach + 1] + band[1, reach - 1].T)
    mixed = jnp.where(upper(block), first, second)
    diagonal = jnp.sum(second * eye(block, block), axis=0, keepdims=True)
    for out in (far, near):
        out[0:block] = mixed
        out[block : 2 * block] = below
        end = (2 + len(cross)) * block
        out[end : end + TILE] = jnp.broadcast_to(diagonal, (TILE, block))
    cols, piece, _ = own.shape
    for c in range(cols):
        group[c] = own[c]
        begin = near.shape[0] + (c - cols) * piece
        near[begin : begin + piece] = own[c]
    kept[0] = first
    kept[1] = below
    kept[2] = second
    is_even = even[0] == 1
    for index, (i, j) in enumerate(cross):
        to_left = band[j, i - j]
        to_right = band[i, 2 * reach + j - i]
        here = slice((2 + index) * block, (3 + index) * block)
        far[here] = jnp.where(is_even, to_left, to_right)
        near[here] = jnp.where(is_even, to_right, to_left)
        kept[3 + index] = to_left
        kept[3 + len(cross) + index] = to_right


def root_kernel(cols, reach, rep_size, even, mask, *refs):
    owns = refs[:rep_size]
    fars = refs[rep_size : 2 * rep_size]
    nears = refs[2 * rep_size : 3 * rep_size]
    y_h, y_l, yt_h, yt_l, p_h, p_l, pt_h, pt_l, unit = refs[3 * rep_size :]
    piece, block = owns[0].shape[1:]
    count = 2 * reach + 1
    window = cols + 2 * reach
    width = count * block
    columns = range(cols)
    is_even = even[0] == 1

    def margin(w):
        parts = []
        for own, far, near in zip(owns, fars, nears):
            if reach <= w < reach + cols:
                parts.append(own[w - reach])
                continue
            index = w if w < reach else w - reach - cols
            from_far = far[far.shape[0] - cols + index]
            if len(near.shape) == 2:
                begin = near.shape[0] + (index - cols) * piece
                from_near = near[begin : begin + piece]
            else:
                from_near = near[index]
            pair = from_far, from_near
            parts.append(jnp.where(is_even, *(pair if w < reach else pair[::-1])))
        return jnp.concatenate(parts, axis=0)

    def at(index):
        return slice(index * block, (index + 1) * block)

    keep = [[mask[c, a].astype(F32) for a in range(count)] for c in columns]
    for w in range(window):
        x = margin(w)
        xt = x.T
        for c in columns:
            a = w - c
            if 0 <= a < count:
                m = keep[c][a]
                y_h[c, :, at(a)], y_l[c, :, at(a)] = split(x * m)
                yt_h[c, at(a), :], yt_l[c, at(a), :] = split(xt * m)

    depth = piece * rep_size
    small_eye = eye(depth, depth)
    gram = [dot3((y_h[c], y_l[c]), (yt_h[c], yt_l[c])) for c in columns]
    gram_s = [split(gram[c]) for c in columns]
    square = [dot3(gram_s[c], gram_s[c]) for c in columns]
    cube = [dot3(gram_s[c], split(square[c])) for c in columns]
    poly = []
    for c in columns:
        sum_sq = width + total(gram[c] * (gram[c] + 2.0 * small_eye))
        s0 = 1.0 / (2.0 * jnp.sqrt(sum_sq / width))
        t0 = 1.5 - 0.5 * s0
        u0 = 1.5 - 0.5 * t0 * t0 * s0
        u1 = 0.5 * t0 * (t0 - s0)
        u2 = 0.5 * (0.25 * s0 - t0)
        u3 = 0.125
        root = jnp.sqrt(s0)
        e1 = (-t0 * u1 - 0.5 * u0) * (root * s0)
        e2 = (-t0 * u2 + 0.5 * u1) * (root * s0 * s0)
        e3 = (-t0 * u3 + 0.5 * u2) * (root * s0 * s0 * s0)
        e4 = 0.5 * u3 * (root * s0 * s0 * s0 * s0)
        unit[c] = jnp.broadcast_to(t0 * u0 * root, unit.shape[1:])
        poly.append(split(e1 * small_eye + e2 * gram[c] + e3 * square[c] + e4 * cube[c]))
    for c in columns:
        p = dot3(poly[c], (y_h[c], y_l[c]))
        p_h[c], p_l[c] = split(p)
        for a in range(count):
            pt_h[c, at(a), :], pt_l[c, at(a), :] = split(p[:, at(a)].T)


def density_kernel(
    cols, reach, rep_size,
    even, mask, fermi, place,
    y_h, y_l, yt_h, yt_l, p_h, p_l, pt_h, pt_l, unit, kept, far, near,
    target,
    ham, ham_h, ham_l, whole, out, sent, *scratch,
):
    prod, shift_h, shift_l, sq_h, sq_l, cross_side, side_h, side_l, tail = (
        scratch[begin : begin + cols] for begin in range(0, 9 * cols, cols)
    )
    depth, width = y_h.shape[1:]
    count = 2 * reach + 1
    block = width // count
    window = cols + 2 * reach
    rows = width // rep_size
    columns = range(cols)
    cross = crossing(reach)
    is_even = even[0] == 1

    def at(index):
        return slice(index * block, (index + 1) * block)

    keep = [[mask[c, a].astype(F32) for a in range(count)] for c in columns]

    half = {}
    for side, base in ((0, 0), (1, reach + cols)):
        def read(index):
            if side == 0:
                return jnp.where(is_even, far[at(index)], near[at(index)])
            return jnp.where(is_even, near[at(index)], far[at(index)])

        end = slice((2 + len(cross)) * block, (2 + len(cross)) * block + 1)
        diagonal = jnp.where(is_even, far[end], near[end]) if side == 0 else jnp.where(is_even, near[end], far[end])
        mixed = read(0)
        one = jnp.where(upper(block), mixed, 0.0)
        two = mixed - one
        half[base, base] = one + two_sided(one, block)
        half[base + 1, base + 1] = two + two.T + diagonal * eye(block, block)
        half[base + 1, base] = read(1)
        for index, (i, j) in enumerate(cross):
            raw = read(2 + index)
            if side == 0:
                half[reach + j, i] = 0.5 * (raw + kept[3 + index].T)
            else:
                half[reach + cols + j, reach + i] = 0.5 * (kept[3 + len(cross) + index] + raw.T)
    half[reach, reach] = kept[0]
    half[reach + 1, reach] = kept[1]
    half[reach + 1, reach + 1] = kept[2]
    for a in range(window):
        for b in range(a + 1):
            if a - b <= reach:
                value = half[a, b]
                ham[at(a), at(b)] = value
                ham_h[at(a), at(b)], ham_l[at(a), at(b)] = split(value)
                if a != b:
                    value = value.T
                    ham[at(b), at(a)] = value
                    ham_h[at(b), at(a)], ham_l[at(b), at(a)] = split(value)
            else:
                none = jnp.zeros((block, block), BF16)
                for i, j in ((a, b), (b, a)):
                    ham_h[at(i), at(j)] = none
                    ham_l[at(i), at(j)] = none

    for c in columns:
        for begin, end in ((0, reach), (reach, reach + 1), (reach + 1, count)):
            low, high = max(0, begin - reach), min(count, end + reach)
            here = slice((c + begin) * block, (c + end) * block), slice((c + low) * block, (c + high) * block)
            inner = slice(low * block, high * block)
            part = dot3((ham_h[here], ham_l[here]), (pt_h[c, inner, :], pt_l[c, inner, :]))
            for a in range(begin, end):
                value = part[at(a - begin)]
                cross_side[c][at(a), :] = value
                side_h[c][at(a), :], side_l[c][at(a), :] = split(value)
    core = [split(dot3((p_h[c], p_l[c]), (side_h[c][...], side_l[c][...]))) for c in columns]
    for c in columns:
        for a in range(count):
            value = (unit[c, 0:1, 0:1] * keep[c][a]) * cross_side[c][at(a), :] + 0.5 * dot3(
                (yt_h[c, at(a), :], yt_l[c, at(a), :]), core[c]
            )
            side_h[c][at(a), :], side_l[c][at(a), :] = split(value)
    for c in columns:
        prod[c][...] = dot3((side_h[c][...], side_l[c][...]), (y_h[c], y_l[c]))

    level = fermi[0] * eye(block, block)
    scale = []
    for c in columns:
        z0 = unit[c, 0:1, 0:1]
        z0_sq = z0 * z0
        sum_sq = jnp.zeros((block, block), F32)
        for a in range(count):
            for b in range(a + 1):
                value = prod[c][at(a), at(b)] + prod[c][at(b), at(a)].T
                if a - b <= reach:
                    value = value + ham[at(c + a), at(c + b)] * (z0_sq * (keep[c][a] * keep[c][b]))
                if a == b:
                    value = value - level
                sum_sq = sum_sq + value * value * (1.0 if a == b else 2.0)
                for i, j in ((a, b), (b, a))[: 1 + (a != b)]:
                    if (i, j) != (a, b):
                        value = value.T
                    if rows % PACKED:
                        whole[c, at(i), at(j)] = value
                    high = value.astype(BF16)
                    shift_h[c][at(i), at(j)] = high
                    shift_l[c][at(i), at(j)] = (2.0 * (value - high.astype(F32))).astype(BF16)
        scale.append(1.0 / (4.0 * (total(sum_sq) / width + 1e-05)))

    edge = width - block
    first = pl.multiple_of(place[0] * rows, rows)
    part_eye = eye(rows, width, first)
    own = pl.ds(first, rows)
    rows_of = [{} for _ in columns]
    copies = []

    def squared(c):
        high, low = shift_h[c][...], shift_l[c][...]
        prod[c][:, :edge] = dot(
            jnp.concatenate([high, high], axis=1),
            jnp.concatenate([high[:, :edge], low[:, :edge]], axis=0),
        )
        tail[c][...] = dot(
            jnp.concatenate([high[edge:], low[edge:]], axis=1), jnp.concatenate([high, high], axis=0)
        )

    def scaled(c):
        factor_c = 0.5 * scale[c]
        for a in range(count):
            for b in range(a + 1):
                if a < count - 1:
                    value = prod[c][at(a), at(b)] + prod[c][at(b), at(a)].T
                elif b < a:
                    value = prod[c][at(a), at(b)] + tail[c][:, at(b)]
                else:
                    value = tail[c][:, at(b)]
                    value = value + value.T
                value = value * factor_c
                sq_h[c][at(a), at(b)], sq_l[c][at(a), at(b)] = split(value)
                if a != b:
                    sq_h[c][at(b), at(a)], sq_l[c][at(b), at(a)] = split(value.T)

    def step(c, source, target_name):
        value = rows_of[c][source]
        rows_of[c][target_name] = 1.5 * value - 0.5 * dot3(split(value), (sq_h[c][...], sq_l[c][...]))

    def start(c):
        if rows % PACKED:
            value = whole[c, own, :]
        else:
            value = shift_h[c][own, :].astype(F32) + 0.5 * shift_l[c][own, :].astype(F32)
        rows_of[c]["x0"] = value * jnp.sqrt(scale[c])
        step(c, "x0", "x1")

    def finish(c):
        left = split(rows_of[c]["y2"])
        for index, begin in enumerate(range(0, width, STEP)):
            here = slice(begin, min(begin + STEP, width))
            y3 = dot3(left, (sq_h[c][:, here], sq_l[c][:, here]))
            out[c, :, here] = 0.5 * (part_eye[:, here] - (1.5 * rows_of[c]["x1"][:, here] - 0.5 * y3))
            copies.append(
                pltpu.make_async_copy(out.at[c, :, here], target.at[c, :, here], sent.at[c, index])
            )
            copies[-1].start()

    stages = [
        squared,
        scaled,
        start,
        lambda c: step(c, "x1", "y1"),
        lambda c: step(c, "y1", "y2"),
        finish,
    ]
    for index in range(len(stages) + cols - 1):
        for c in columns:
            if 0 <= index - c < len(stages):
                stages[index - c](c)
    for copy in copies:
        copy.wait()


def column_kernel(cols, reach, rep_size, even, mask, fermi, place, *refs):
    inputs = 3 * rep_size
    pieces, (kept, far, target) = refs[:inputs], refs[inputs : inputs + 3]
    root, scratch = refs[inputs + 3 : inputs + 12], refs[inputs + 12 :]
    root_kernel(cols, reach, rep_size, even, mask, *pieces, *root)
    density_kernel(
        cols, reach, rep_size, even, mask, fermi, place,
        *root, kept, far, pieces[2 * rep_size], target, *scratch,
    )


def two_sided(one, block):
    return jnp.where(upper(block), 0.0, one.T)


def shaped(*shape, dtype=F32):
    return jax.ShapeDtypeStruct(shape, dtype)


SMEM = pl.BlockSpec(memory_space=pltpu.SMEM)
VMEM = pl.BlockSpec(memory_space=pltpu.VMEM)


def edges(even, band, own):
    cols, count, block, _ = band.shape
    reach = (count - 1) // 2
    cross = len(crossing(reach))
    height = (2 + cross) * block + TILE
    return pl.pallas_call(
        functools.partial(edge_kernel, reach),
        out_shape=[shaped(height, block), shaped(height + own.shape[0] * own.shape[1], block), shaped(3 + 2 * cross, block, block), shaped(cols, *own.shape[1:])],
        in_specs=[SMEM, VMEM, VMEM],
        out_specs=[VMEM] * 4,
        compiler_params=pltpu.CompilerParams(vmem_limit_bytes=8 * 2**20),
        cost_estimate=pl.CostEstimate(flops=0, bytes_accessed=4 * 2**20, transcendentals=0),
    )(even, band, own)


def density(even, mask, fermi, place, owns, fars, nears, kept, far, reach):
    rep_size = len(owns)
    cols, piece, block = owns[0].shape
    depth = piece * rep_size
    width = (2 * reach + 1) * block
    rows = width // rep_size
    window = (cols + 2 * reach) * block
    return pl.pallas_call(
        functools.partial(column_kernel, cols, reach, rep_size),
        out_shape=shaped(cols, rows, width),
        in_specs=[SMEM] * 4 + [VMEM] * (3 * rep_size + 2),
        out_specs=pl.BlockSpec(memory_space=pl.ANY),
        scratch_shapes=[
            *[pltpu.VMEM((cols, depth, width), BF16)] * 2,
            *[pltpu.VMEM((cols, width, depth), BF16)] * 2,
            *[pltpu.VMEM((cols, depth, width), BF16)] * 2,
            *[pltpu.VMEM((cols, width, depth), BF16)] * 2,
            pltpu.VMEM((cols, TILE, block), F32),
            pltpu.VMEM((window, window), F32),
            pltpu.VMEM((window, window), BF16),
            pltpu.VMEM((window, window), BF16),
            pltpu.VMEM((cols, width, width) if rows % PACKED else (1, TILE, block), F32),
            pltpu.VMEM((cols, rows, width), F32),
            pltpu.SemaphoreType.DMA((cols, pl.cdiv(width, STEP))),
            *[pltpu.VMEM((width, width), F32)] * cols,
            *[pltpu.VMEM((width, width), BF16)] * (4 * cols),
            *[pltpu.VMEM((width, depth), F32)] * cols,
            *[pltpu.VMEM((width, depth), BF16)] * (2 * cols),
            *[pltpu.VMEM((block, width), F32)] * cols,
        ],
        compiler_params=pltpu.CompilerParams(vmem_limit_bytes=36 * 2**20),
        cost_estimate=pl.CostEstimate(flops=2**34, bytes_accessed=8 * 2**20, transcendentals=0),
    )(even, mask, fermi, place, *owns, *fars, *nears, kept, far)


def near_swap(value):
    return lax.ppermute(value, "cols", [(i, i ^ 1) for i in range(lax.axis_size("cols"))])


def far_swap(value):
    count = lax.axis_size("cols")
    return lax.ppermute(value, "cols", [(i, (((i + 1) ^ 1) - 1) % count) for i in range(count)])


def rep_swap(value, step):
    return lax.ppermute(value, "rep", [(i, i ^ step) for i in range(lax.axis_size("rep"))])


def on_device(hamiltonian_band, margin_factors, neighbour_mask, fermi_level):
    cols, count, _, _ = hamiltonian_band.shape
    reach = (count - 1) // 2
    rep_size = lax.axis_size("rep")
    even = 1 - (lax.axis_index("cols").astype(jnp.int32) % 2).reshape(1)
    place = lax.axis_index("rep").astype(jnp.int32).reshape(1)
    margin_far = far_swap(margin_factors)
    to_far, to_near, kept, own = edges(even, hamiltonian_band, margin_factors)
    far = far_swap(to_far)
    near = near_swap(to_near)
    group = jnp.concatenate([own, margin_far], axis=0)
    groups = [group] + [rep_swap(group, step) for step in range(1, rep_size)]
    owns = [own] + groups[1:]
    fars = [margin_far] + groups[1:]
    nears = [near] + [near_swap(value) for value in groups[1:]]
    return density(even, neighbour_mask, fermi_level, place, owns, fars, nears, kept, far, reach)


def solution(mesh):
    in_specs = (P("cols", None, None, None), P("cols", "rep", None), P("cols", None), P())
    out_specs = P("cols", "rep", None)
    return jax.shard_map(
        on_device, mesh=mesh, in_specs=in_specs, out_specs=out_specs, check_vma=False
    )
```

```python
import functools

import jax
import jax.numpy as jnp
from jax import lax
from jax.experimental import pallas as pl
from jax.experimental.pallas import tpu as pltpu
from jax.sharding import PartitionSpec as P

F32 = jnp.float32
BF16 = jnp.bfloat16
PACKED = 16
STEP = 256
TILE = 8


def split(value):
    high = value.astype(BF16)
    return high, (value - high.astype(F32)).astype(BF16)


def dot(left, right):
    return jnp.dot(left, right, preferred_element_type=F32)


def dot3(left, right):
    (left_high, left_low), (right_high, right_low) = left, right
    return dot(
        jnp.concatenate([left_high, left_low, left_high], axis=1),
        jnp.concatenate([right_high, right_high, right_low], axis=0),
    )


def total(value):
    return jnp.sum(jnp.sum(value, axis=0, keepdims=True), axis=1, keepdims=True)


def eye(rows, columns, first=0):
    row = lax.broadcasted_iota(jnp.int32, (rows, columns), 0) + first
    column = lax.broadcasted_iota(jnp.int32, (rows, columns), 1)
    return jnp.where(row == column, 1.0, 0.0).astype(F32)


def upper(block):
    row = lax.broadcasted_iota(jnp.int32, (block, block), 0)
    return row <= lax.broadcasted_iota(jnp.int32, (block, block), 1)


def crossing(reach):
    return [(i, j) for j in range(reach) for i in range(reach) if reach + j - i <= reach]


def edge_kernel(reach, even, mask, band, own, far, near, kept, group, flags):
    block = band.shape[2]
    cross = crossing(reach)
    first = 0.5 * (band[0, reach] + band[0, reach].T)
    second = 0.5 * (band[1, reach] + band[1, reach].T)
    below = 0.5 * (band[0, reach + 1] + band[1, reach - 1].T)
    mixed = jnp.where(upper(block), first, second)
    diagonal = jnp.sum(second * eye(block, block), axis=0, keepdims=True)
    for out in (far, near):
        out[0:block] = mixed
        out[block : 2 * block] = below
        end = (2 + len(cross)) * block
        out[end : end + TILE] = jnp.broadcast_to(diagonal, (TILE, block))
    cols, piece, _ = own.shape
    for c in range(cols):
        group[c] = own[c]
        begin = near.shape[0] + (c - cols) * piece
        near[begin : begin + piece] = own[c]
    flags[...] = mask[...].astype(F32)
    kept[0] = first
    kept[1] = below
    kept[2] = second
    is_even = even[0] == 1
    for index, (i, j) in enumerate(cross):
        to_left = band[j, i - j]
        to_right = band[i, 2 * reach + j - i]
        here = slice((2 + index) * block, (3 + index) * block)
        far[here] = jnp.where(is_even, to_left, to_right)
        near[here] = jnp.where(is_even, to_right, to_left)
        kept[3 + index] = to_left
        kept[3 + len(cross) + index] = to_right


def root_kernel(cols, reach, rep_size, even, mask, *refs):
    owns = refs[:rep_size]
    fars = refs[rep_size : 2 * rep_size]
    nears = refs[2 * rep_size : 3 * rep_size]
    y_h, y_l, yt_h, yt_l, p_h, p_l, pt_h, pt_l, unit = refs[3 * rep_size :]
    piece, block = owns[0].shape[1:]
    count = 2 * reach + 1
    window = cols + 2 * reach
    width = count * block
    columns = range(cols)
    is_even = even[0] == 1

    def margin(w):
        parts = []
        for own, far, near in zip(owns, fars, nears):
            if reach <= w < reach + cols:
                parts.append(own[w - reach])
                continue
            index = w if w < reach else w - reach - cols
            from_far = far[far.shape[0] - cols + index]
            if len(near.shape) == 2:
                begin = near.shape[0] + (index - cols) * piece
                from_near = near[begin : begin + piece]
            else:
                from_near = near[index]
            pair = from_far, from_near
            parts.append(jnp.where(is_even, *(pair if w < reach else pair[::-1])))
        return jnp.concatenate(parts, axis=0)

    def at(index):
        return slice(index * block, (index + 1) * block)

    keep = [[mask[c : c + 1, a : a + 1] for a in range(count)] for c in columns]
    for w in range(window):
        x = margin(w)
        xt = x.T
        for c in columns:
            a = w - c
            if 0 <= a < count:
                m = keep[c][a]
                y_h[c, :, at(a)], y_l[c, :, at(a)] = split(x * m)
                yt_h[c, at(a), :], yt_l[c, at(a), :] = split(xt * m)

    depth = piece * rep_size
    small_eye = eye(depth, depth)
    gram = [dot3((y_h[c], y_l[c]), (yt_h[c], yt_l[c])) for c in columns]
    gram_s = [split(gram[c]) for c in columns]
    square = [dot3(gram_s[c], gram_s[c]) for c in columns]
    cube = [dot3(gram_s[c], split(square[c])) for c in columns]
    poly = []
    for c in columns:
        sum_sq = width + total(gram[c] * (gram[c] + 2.0 * small_eye))
        s0 = 1.0 / (2.0 * jnp.sqrt(sum_sq / width))
        t0 = 1.5 - 0.5 * s0
        u0 = 1.5 - 0.5 * t0 * t0 * s0
        u1 = 0.5 * t0 * (t0 - s0)
        u2 = 0.5 * (0.25 * s0 - t0)
        u3 = 0.125
        root = jnp.sqrt(s0)
        e1 = (-t0 * u1 - 0.5 * u0) * (root * s0)
        e2 = (-t0 * u2 + 0.5 * u1) * (root * s0 * s0)
        e3 = (-t0 * u3 + 0.5 * u2) * (root * s0 * s0 * s0)
        e4 = 0.5 * u3 * (root * s0 * s0 * s0 * s0)
        unit[c] = jnp.broadcast_to(t0 * u0 * root, unit.shape[1:])
        poly.append(split(e1 * small_eye + e2 * gram[c] + e3 * square[c] + e4 * cube[c]))
    for c in columns:
        p = dot3(poly[c], (y_h[c], y_l[c]))
        p_h[c], p_l[c] = split(p)
        for a in range(count):
            pt_h[c, at(a), :], pt_l[c, at(a), :] = split(p[:, at(a)].T)


def density_kernel(
    cols, reach, rep_size,
    even, mask, fermi, place,
    y_h, y_l, yt_h, yt_l, p_h, p_l, pt_h, pt_l, unit, kept, far, near,
    target,
    ham, ham_h, ham_l, whole, out, sent, *scratch,
):
    prod, shift_h, shift_l, sq_h, sq_l, cross_side, side_h, side_l, tail = (
        scratch[begin : begin + cols] for begin in range(0, 9 * cols, cols)
    )
    depth, width = y_h.shape[1:]
    count = 2 * reach + 1
    block = width // count
    window = cols + 2 * reach
    rows = width // rep_size
    columns = range(cols)
    cross = crossing(reach)
    is_even = even[0] == 1

    def at(index):
        return slice(index * block, (index + 1) * block)

    keep = [[mask[c : c + 1, a : a + 1] for a in range(count)] for c in columns]

    half = {}
    for side, base in ((0, 0), (1, reach + cols)):
        def read(index):
            if side == 0:
                return jnp.where(is_even, far[at(index)], near[at(index)])
            return jnp.where(is_even, near[at(index)], far[at(index)])

        end = slice((2 + len(cross)) * block, (2 + len(cross)) * block + 1)
        diagonal = jnp.where(is_even, far[end], near[end]) if side == 0 else jnp.where(is_even, near[end], far[end])
        mixed = read(0)
        one = jnp.where(upper(block), mixed, 0.0)
        two = mixed - one
        half[base, base] = one + two_sided(one, block)
        half[base + 1, base + 1] = two + two.T + diagonal * eye(block, block)
        half[base + 1, base] = read(1)
        for index, (i, j) in enumerate(cross):
            raw = read(2 + index)
            if side == 0:
                half[reach + j, i] = 0.5 * (raw + kept[3 + index].T)
            else:
                half[reach + cols + j, reach + i] = 0.5 * (kept[3 + len(cross) + index] + raw.T)
    half[reach, reach] = kept[0]
    half[reach + 1, reach] = kept[1]
    half[reach + 1, reach + 1] = kept[2]
    for a in range(window):
        for b in range(a + 1):
            if a - b <= reach:
                value = half[a, b]
                ham[at(a), at(b)] = value
                ham_h[at(a), at(b)], ham_l[at(a), at(b)] = split(value)
                if a != b:
                    value = value.T
                    ham[at(b), at(a)] = value
                    ham_h[at(b), at(a)], ham_l[at(b), at(a)] = split(value)
            else:
                none = jnp.zeros((block, block), BF16)
                for i, j in ((a, b), (b, a)):
                    ham_h[at(i), at(j)] = none
                    ham_l[at(i), at(j)] = none

    for c in columns:
        for begin, end in ((0, reach), (reach, reach + 1), (reach + 1, count)):
            low, high = max(0, begin - reach), min(count, end + reach)
            here = slice((c + begin) * block, (c + end) * block), slice((c + low) * block, (c + high) * block)
            inner = slice(low * block, high * block)
            part = dot3((ham_h[here], ham_l[here]), (pt_h[c, inner, :], pt_l[c, inner, :]))
            for a in range(begin, end):
                value = part[at(a - begin)]
                cross_side[c][at(a), :] = value
                side_h[c][at(a), :], side_l[c][at(a), :] = split(value)
    core = [split(dot3((p_h[c], p_l[c]), (side_h[c][...], side_l[c][...]))) for c in columns]
    for c in columns:
        for a in range(count):
            value = (unit[c, 0:1, 0:1] * keep[c][a]) * cross_side[c][at(a), :] + 0.5 * dot3(
                (yt_h[c, at(a), :], yt_l[c, at(a), :]), core[c]
            )
            side_h[c][at(a), :], side_l[c][at(a), :] = split(value)
    for c in columns:
        prod[c][...] = dot3((side_h[c][...], side_l[c][...]), (y_h[c], y_l[c]))

    level = fermi[0] * eye(block, block)
    scale = []
    for c in columns:
        z0 = unit[c, 0:1, 0:1]
        z0_sq = z0 * z0
        sum_sq = jnp.zeros((block, block), F32)
        for a in range(count):
            for b in range(a + 1):
                value = prod[c][at(a), at(b)] + prod[c][at(b), at(a)].T
                if a - b <= reach:
                    value = value + ham[at(c + a), at(c + b)] * (z0_sq * (keep[c][a] * keep[c][b]))
                if a == b:
                    value = value - level
                sum_sq = sum_sq + value * value * (1.0 if a == b else 2.0)
                for i, j in ((a, b), (b, a))[: 1 + (a != b)]:
                    if (i, j) != (a, b):
                        value = value.T
                    if rows % PACKED:
                        whole[c, at(i), at(j)] = value
                    high = value.astype(BF16)
                    shift_h[c][at(i), at(j)] = high
                    shift_l[c][at(i), at(j)] = (2.0 * (value - high.astype(F32))).astype(BF16)
        scale.append(1.0 / (4.0 * (total(sum_sq) / width + 1e-05)))

    edge = width - block
    first = pl.multiple_of(place[0] * rows, rows)
    part_eye = eye(rows, width, first)
    own = pl.ds(first, rows)
    rows_of = [{} for _ in columns]
    copies = []

    def squared(c):
        high, low = shift_h[c][...], shift_l[c][...]
        prod[c][:, :edge] = dot(
            jnp.concatenate([high, high], axis=1),
            jnp.concatenate([high[:, :edge], low[:, :edge]], axis=0),
        )
        tail[c][...] = dot(
            jnp.concatenate([high[edge:], low[edge:]], axis=1), jnp.concatenate([high, high], axis=0)
        )

    def scaled(c):
        factor_c = 0.5 * scale[c]
        for a in range(count):
            for b in range(a + 1):
                if a < count - 1:
                    value = prod[c][at(a), at(b)] + prod[c][at(b), at(a)].T
                elif b < a:
                    value = prod[c][at(a), at(b)] + tail[c][:, at(b)]
                else:
                    value = tail[c][:, at(b)]
                    value = value + value.T
                value = value * factor_c
                sq_h[c][at(a), at(b)], sq_l[c][at(a), at(b)] = split(value)
                if a != b:
                    sq_h[c][at(b), at(a)], sq_l[c][at(b), at(a)] = split(value.T)

    def step(c, source, target_name):
        value = rows_of[c][source]
        rows_of[c][target_name] = 1.5 * value - 0.5 * dot3(split(value), (sq_h[c][...], sq_l[c][...]))

    def start(c):
        if rows % PACKED:
            value = whole[c, own, :]
        else:
            value = shift_h[c][own, :].astype(F32) + 0.5 * shift_l[c][own, :].astype(F32)
        rows_of[c]["x0"] = value * jnp.sqrt(scale[c])
        step(c, "x0", "x1")

    def finish(c):
        left = split(rows_of[c]["y2"])
        for index, begin in enumerate(range(0, width, STEP)):
            here = slice(begin, min(begin + STEP, width))
            y3 = dot3(left, (sq_h[c][:, here], sq_l[c][:, here]))
            out[c, :, here] = 0.5 * (part_eye[:, here] - (1.5 * rows_of[c]["x1"][:, here] - 0.5 * y3))
            copies.append(
                pltpu.make_async_copy(out.at[c, :, here], target.at[c, :, here], sent.at[c, index])
            )
            copies[-1].start()

    stages = [
        squared,
        scaled,
        start,
        lambda c: step(c, "x1", "y1"),
        lambda c: step(c, "y1", "y2"),
        finish,
    ]
    for index in range(len(stages) + cols - 1):
        for c in columns:
            if 0 <= index - c < len(stages):
                stages[index - c](c)
    for copy in copies:
        copy.wait()


def column_kernel(cols, reach, rep_size, even, mask, fermi, place, *refs):
    inputs = 3 * rep_size
    pieces, (kept, far, target) = refs[:inputs], refs[inputs : inputs + 3]
    root, scratch = refs[inputs + 3 : inputs + 12], refs[inputs + 12 :]
    root_kernel(cols, reach, rep_size, even, mask, *pieces, *root)
    density_kernel(
        cols, reach, rep_size, even, mask, fermi, place,
        *root, kept, far, pieces[2 * rep_size], target, *scratch,
    )


def two_sided(one, block):
    return jnp.where(upper(block), 0.0, one.T)


def shaped(*shape, dtype=F32):
    return jax.ShapeDtypeStruct(shape, dtype)


SMEM = pl.BlockSpec(memory_space=pltpu.SMEM)
VMEM = pl.BlockSpec(memory_space=pltpu.VMEM)


def edges(even, mask, band, own):
    cols, count, block, _ = band.shape
    reach = (count - 1) // 2
    cross = len(crossing(reach))
    height = (2 + cross) * block + TILE
    return pl.pallas_call(
        functools.partial(edge_kernel, reach),
        out_shape=[shaped(height, block), shaped(height + own.shape[0] * own.shape[1], block), shaped(3 + 2 * cross, block, block), shaped(cols, *own.shape[1:]), shaped(*mask.shape)],
        in_specs=[SMEM, VMEM, VMEM, VMEM],
        out_specs=[VMEM] * 5,
        compiler_params=pltpu.CompilerParams(vmem_limit_bytes=8 * 2**20),
        cost_estimate=pl.CostEstimate(flops=0, bytes_accessed=4 * 2**20, transcendentals=0),
    )(even, mask, band, own)


def density(even, mask, fermi, place, owns, fars, nears, kept, far, reach):
    rep_size = len(owns)
    cols, piece, block = owns[0].shape
    depth = piece * rep_size
    width = (2 * reach + 1) * block
    rows = width // rep_size
    window = (cols + 2 * reach) * block
    return pl.pallas_call(
        functools.partial(column_kernel, cols, reach, rep_size),
        out_shape=shaped(cols, rows, width),
        in_specs=[SMEM, VMEM, SMEM, SMEM] + [VMEM] * (3 * rep_size + 2),
        out_specs=pl.BlockSpec(memory_space=pl.ANY),
        scratch_shapes=[
            *[pltpu.VMEM((cols, depth, width), BF16)] * 2,
            *[pltpu.VMEM((cols, width, depth), BF16)] * 2,
            *[pltpu.VMEM((cols, depth, width), BF16)] * 2,
            *[pltpu.VMEM((cols, width, depth), BF16)] * 2,
            pltpu.VMEM((cols, TILE, block), F32),
            pltpu.VMEM((window, window), F32),
            pltpu.VMEM((window, window), BF16),
            pltpu.VMEM((window, window), BF16),
            pltpu.VMEM((cols, width, width) if rows % PACKED else (1, TILE, block), F32),
            pltpu.VMEM((cols, rows, width), F32),
            pltpu.SemaphoreType.DMA((cols, pl.cdiv(width, STEP))),
            *[pltpu.VMEM((width, width), F32)] * cols,
            *[pltpu.VMEM((width, width), BF16)] * (4 * cols),
            *[pltpu.VMEM((width, depth), F32)] * cols,
            *[pltpu.VMEM((width, depth), BF16)] * (2 * cols),
            *[pltpu.VMEM((block, width), F32)] * cols,
        ],
        compiler_params=pltpu.CompilerParams(vmem_limit_bytes=36 * 2**20),
        cost_estimate=pl.CostEstimate(flops=2**34, bytes_accessed=8 * 2**20, transcendentals=0),
    )(even, mask, fermi, place, *owns, *fars, *nears, kept, far)


def near_swap(value):
    return lax.ppermute(value, "cols", [(i, i ^ 1) for i in range(lax.axis_size("cols"))])


def far_swap(value):
    count = lax.axis_size("cols")
    return lax.ppermute(value, "cols", [(i, (((i + 1) ^ 1) - 1) % count) for i in range(count)])


def rep_swap(value, step):
    return lax.ppermute(value, "rep", [(i, i ^ step) for i in range(lax.axis_size("rep"))])


def on_device(hamiltonian_band, margin_factors, neighbour_mask, fermi_level):
    cols, count, _, _ = hamiltonian_band.shape
    reach = (count - 1) // 2
    rep_size = lax.axis_size("rep")
    even = 1 - (lax.axis_index("cols").astype(jnp.int32) % 2).reshape(1)
    place = lax.axis_index("rep").astype(jnp.int32).reshape(1)
    margin_far = far_swap(margin_factors)
    to_far, to_near, kept, own, flags = edges(even, neighbour_mask, hamiltonian_band, margin_factors)
    far = far_swap(to_far)
    near = near_swap(to_near)
    group = jnp.concatenate([own, margin_far], axis=0)
    groups = [group] + [rep_swap(group, step) for step in range(1, rep_size)]
    owns = [own] + groups[1:]
    fars = [margin_far] + groups[1:]
    nears = [near] + [near_swap(value) for value in groups[1:]]
    return density(even, flags, fermi_level, place, owns, fars, nears, kept, far, reach)


def solution(mesh):
    in_specs = (P("cols", None, None, None), P("cols", "rep", None), P("cols", None), P())
    out_specs = P("cols", "rep", None)
    return jax.shard_map(
        on_device, mesh=mesh, in_specs=in_specs, out_specs=out_specs, check_vma=False
    )
```

```python
import functools

import jax
import jax.numpy as jnp
from jax import lax
from jax.experimental import pallas as pl
from jax.experimental.pallas import tpu as pltpu
from jax.sharding import PartitionSpec as P

F32 = jnp.float32
BF16 = jnp.bfloat16
PACKED = 16
STEP = 256
TILE = 8


def split(value):
    high = value.astype(BF16)
    return high, (value - high.astype(F32)).astype(BF16)


def dot(left, right):
    return jnp.dot(left, right, preferred_element_type=F32)


def dot3(left, right):
    (left_high, left_low), (right_high, right_low) = left, right
    return dot(
        jnp.concatenate([left_high, left_low, left_high], axis=1),
        jnp.concatenate([right_high, right_high, right_low], axis=0),
    )


def total(value):
    return jnp.sum(jnp.sum(value, axis=0, keepdims=True), axis=1, keepdims=True)


def eye(rows, columns, first=0):
    row = lax.broadcasted_iota(jnp.int32, (rows, columns), 0) + first
    column = lax.broadcasted_iota(jnp.int32, (rows, columns), 1)
    return jnp.where(row == column, 1.0, 0.0).astype(F32)


def upper(block):
    row = lax.broadcasted_iota(jnp.int32, (block, block), 0)
    return row <= lax.broadcasted_iota(jnp.int32, (block, block), 1)


def crossing(reach):
    return [(i, j) for j in range(reach) for i in range(reach) if reach + j - i <= reach]


def edge_kernel(reach, even, mask, band, own, far, near, kept, group, flags):
    block = band.shape[2]
    cross = crossing(reach)
    first = 0.5 * (band[0, reach] + band[0, reach].T)
    second = 0.5 * (band[1, reach] + band[1, reach].T)
    below = 0.5 * (band[0, reach + 1] + band[1, reach - 1].T)
    mixed = jnp.where(upper(block), first, second)
    diagonal = jnp.sum(second * eye(block, block), axis=0, keepdims=True)
    for out in (far, near):
        out[0:block] = mixed
        out[block : 2 * block] = below
        end = (2 + len(cross)) * block
        out[end : end + TILE] = jnp.broadcast_to(diagonal, (TILE, block))
    cols, piece, _ = own.shape
    for c in range(cols):
        group[c] = own[c]
        begin = near.shape[0] + (c - cols) * piece
        near[begin : begin + piece] = own[c]
    flags[...] = mask[...].astype(F32)
    kept[0] = first
    kept[1] = below
    kept[2] = second
    is_even = even[0] == 1
    for index, (i, j) in enumerate(cross):
        to_left = band[j, i - j]
        to_right = band[i, 2 * reach + j - i]
        here = slice((2 + index) * block, (3 + index) * block)
        far[here] = jnp.where(is_even, to_left, to_right)
        near[here] = jnp.where(is_even, to_right, to_left)
        kept[3 + index] = to_left
        kept[3 + len(cross) + index] = to_right


def root_kernel(cols, reach, rep_size, even, mask, *refs):
    owns = refs[:rep_size]
    fars = refs[rep_size : 2 * rep_size]
    nears = refs[2 * rep_size : 3 * rep_size]
    y_h, y_l, yt_h, yt_l, p_h, p_l, pt_h, pt_l, unit = refs[3 * rep_size :]
    piece, block = owns[0].shape[1:]
    count = 2 * reach + 1
    window = cols + 2 * reach
    width = count * block
    columns = range(cols)
    is_even = even[0] == 1

    def margin(w):
        parts = []
        for own, far, near in zip(owns, fars, nears):
            if reach <= w < reach + cols:
                parts.append(own[w - reach])
                continue
            index = w if w < reach else w - reach - cols
            from_far = far[far.shape[0] - cols + index]
            if len(near.shape) == 2:
                begin = near.shape[0] + (index - cols) * piece
                from_near = near[begin : begin + piece]
            else:
                from_near = near[index]
            pair = from_far, from_near
            parts.append(jnp.where(is_even, *(pair if w < reach else pair[::-1])))
        return jnp.concatenate(parts, axis=0)

    def at(index):
        return slice(index * block, (index + 1) * block)

    keep = [[mask[c : c + 1, a : a + 1] for a in range(count)] for c in columns]
    for w in range(window):
        x = margin(w)
        xt = x.T
        x_s, xt_s = split(x), split(xt)
        for c in columns:
            a = w - c
            if 0 <= a < count:
                wide = jnp.broadcast_to(keep[c][a], (1, block)).astype(BF16)
                tall = jnp.broadcast_to(keep[c][a], (1, xt.shape[1])).astype(BF16)
                y_h[c, :, at(a)], y_l[c, :, at(a)] = x_s[0] * wide, x_s[1] * wide
                yt_h[c, at(a), :], yt_l[c, at(a), :] = xt_s[0] * tall, xt_s[1] * tall

    depth = piece * rep_size
    small_eye = eye(depth, depth)
    gram = [dot3((y_h[c], y_l[c]), (yt_h[c], yt_l[c])) for c in columns]
    gram_s = [split(gram[c]) for c in columns]
    square = [dot3(gram_s[c], gram_s[c]) for c in columns]
    cube = [dot3(gram_s[c], split(square[c])) for c in columns]
    poly = []
    for c in columns:
        sum_sq = width + total(gram[c] * (gram[c] + 2.0 * small_eye))
        s0 = 1.0 / (2.0 * jnp.sqrt(sum_sq / width))
        t0 = 1.5 - 0.5 * s0
        u0 = 1.5 - 0.5 * t0 * t0 * s0
        u1 = 0.5 * t0 * (t0 - s0)
        u2 = 0.5 * (0.25 * s0 - t0)
        u3 = 0.125
        root = jnp.sqrt(s0)
        e1 = (-t0 * u1 - 0.5 * u0) * (root * s0)
        e2 = (-t0 * u2 + 0.5 * u1) * (root * s0 * s0)
        e3 = (-t0 * u3 + 0.5 * u2) * (root * s0 * s0 * s0)
        e4 = 0.5 * u3 * (root * s0 * s0 * s0 * s0)
        unit[c] = jnp.broadcast_to(t0 * u0 * root, unit.shape[1:])
        poly.append(split(e1 * small_eye + e2 * gram[c] + e3 * square[c] + e4 * cube[c]))
    for c in columns:
        p = dot3(poly[c], (y_h[c], y_l[c]))
        p_h[c], p_l[c] = split(p)
        for a in range(count):
            pt_h[c, at(a), :], pt_l[c, at(a), :] = split(p[:, at(a)].T)


def density_kernel(
    cols, reach, rep_size,
    even, mask, fermi, place,
    y_h, y_l, yt_h, yt_l, p_h, p_l, pt_h, pt_l, unit, kept, far, near,
    target,
    ham, ham_h, ham_l, whole, out, sent, *scratch,
):
    prod, shift_h, shift_l, sq_h, sq_l, cross_side, side_h, side_l, tail = (
        scratch[begin : begin + cols] for begin in range(0, 9 * cols, cols)
    )
    depth, width = y_h.shape[1:]
    count = 2 * reach + 1
    block = width // count
    window = cols + 2 * reach
    rows = width // rep_size
    columns = range(cols)
    cross = crossing(reach)
    is_even = even[0] == 1

    def at(index):
        return slice(index * block, (index + 1) * block)

    keep = [[mask[c : c + 1, a : a + 1] for a in range(count)] for c in columns]

    half = {}
    for side, base in ((0, 0), (1, reach + cols)):
        def read(index):
            if side == 0:
                return jnp.where(is_even, far[at(index)], near[at(index)])
            return jnp.where(is_even, near[at(index)], far[at(index)])

        end = slice((2 + len(cross)) * block, (2 + len(cross)) * block + 1)
        diagonal = jnp.where(is_even, far[end], near[end]) if side == 0 else jnp.where(is_even, near[end], far[end])
        mixed = read(0)
        one = jnp.where(upper(block), mixed, 0.0)
        two = mixed - one
        half[base, base] = one + two_sided(one, block)
        half[base + 1, base + 1] = two + two.T + diagonal * eye(block, block)
        half[base + 1, base] = read(1)
        for index, (i, j) in enumerate(cross):
            raw = read(2 + index)
            if side == 0:
                half[reach + j, i] = 0.5 * (raw + kept[3 + index].T)
            else:
                half[reach + cols + j, reach + i] = 0.5 * (kept[3 + len(cross) + index] + raw.T)
    half[reach, reach] = kept[0]
    half[reach + 1, reach] = kept[1]
    half[reach + 1, reach + 1] = kept[2]
    for a in range(window):
        for b in range(a + 1):
            if a - b <= reach:
                value = half[a, b]
                ham[at(a), at(b)] = value
                ham_h[at(a), at(b)], ham_l[at(a), at(b)] = split(value)
                if a != b:
                    value = value.T
                    ham[at(b), at(a)] = value
                    ham_h[at(b), at(a)], ham_l[at(b), at(a)] = split(value)
            else:
                none = jnp.zeros((block, block), BF16)
                for i, j in ((a, b), (b, a)):
                    ham_h[at(i), at(j)] = none
                    ham_l[at(i), at(j)] = none

    for c in columns:
        for begin, end in ((0, reach), (reach, reach + 1), (reach + 1, count)):
            low, high = max(0, begin - reach), min(count, end + reach)
            here = slice((c + begin) * block, (c + end) * block), slice((c + low) * block, (c + high) * block)
            inner = slice(low * block, high * block)
            part = dot3((ham_h[here], ham_l[here]), (pt_h[c, inner, :], pt_l[c, inner, :]))
            for a in range(begin, end):
                value = part[at(a - begin)]
                cross_side[c][at(a), :] = value
                side_h[c][at(a), :], side_l[c][at(a), :] = split(value)
    core = [split(dot3((p_h[c], p_l[c]), (side_h[c][...], side_l[c][...]))) for c in columns]
    for c in columns:
        for a in range(count):
            value = (unit[c, 0:1, 0:1] * keep[c][a]) * cross_side[c][at(a), :] + 0.5 * dot3(
                (yt_h[c, at(a), :], yt_l[c, at(a), :]), core[c]
            )
            side_h[c][at(a), :], side_l[c][at(a), :] = split(value)
    for c in columns:
        prod[c][...] = dot3((side_h[c][...], side_l[c][...]), (y_h[c], y_l[c]))

    level = fermi[0] * eye(block, block)
    scale = []
    for c in columns:
        z0 = unit[c, 0:1, 0:1]
        z0_sq = z0 * z0
        sum_sq = jnp.zeros((block, block), F32)
        for a in range(count):
            for b in range(a + 1):
                value = prod[c][at(a), at(b)] + prod[c][at(b), at(a)].T
                if a - b <= reach:
                    value = value + ham[at(c + a), at(c + b)] * (z0_sq * (keep[c][a] * keep[c][b]))
                if a == b:
                    value = value - level
                sum_sq = sum_sq + value * value * (1.0 if a == b else 2.0)
                for i, j in ((a, b), (b, a))[: 1 + (a != b)]:
                    if (i, j) != (a, b):
                        value = value.T
                    if rows % PACKED:
                        whole[c, at(i), at(j)] = value
                    high = value.astype(BF16)
                    shift_h[c][at(i), at(j)] = high
                    shift_l[c][at(i), at(j)] = (2.0 * (value - high.astype(F32))).astype(BF16)
        scale.append(1.0 / (4.0 * (total(sum_sq) / width + 1e-05)))

    edge = width - block
    first = pl.multiple_of(place[0] * rows, rows)
    part_eye = eye(rows, width, first)
    own = pl.ds(first, rows)
    rows_of = [{} for _ in columns]
    copies = []

    def squared(c):
        high, low = shift_h[c][...], shift_l[c][...]
        prod[c][:, :edge] = dot(
            jnp.concatenate([high, high], axis=1),
            jnp.concatenate([high[:, :edge], low[:, :edge]], axis=0),
        )
        tail[c][...] = dot(
            jnp.concatenate([high[edge:], low[edge:]], axis=1), jnp.concatenate([high, high], axis=0)
        )

    def scaled(c):
        factor_c = 0.5 * scale[c]
        for a in range(count):
            for b in range(a + 1):
                if a < count - 1:
                    value = prod[c][at(a), at(b)] + prod[c][at(b), at(a)].T
                elif b < a:
                    value = prod[c][at(a), at(b)] + tail[c][:, at(b)]
                else:
                    value = tail[c][:, at(b)]
                    value = value + value.T
                value = value * factor_c
                sq_h[c][at(a), at(b)], sq_l[c][at(a), at(b)] = split(value)
                if a != b:
                    sq_h[c][at(b), at(a)], sq_l[c][at(b), at(a)] = split(value.T)

    def step(c, source, target_name):
        value = rows_of[c][source]
        rows_of[c][target_name] = 1.5 * value - 0.5 * dot3(split(value), (sq_h[c][...], sq_l[c][...]))

    def start(c):
        if rows % PACKED:
            value = whole[c, own, :]
        else:
            value = shift_h[c][own, :].astype(F32) + 0.5 * shift_l[c][own, :].astype(F32)
        rows_of[c]["x0"] = value * jnp.sqrt(scale[c])
        step(c, "x0", "x1")

    def finish(c):
        left = split(rows_of[c]["y2"])
        for index, begin in enumerate(range(0, width, STEP)):
            here = slice(begin, min(begin + STEP, width))
            y3 = dot3(left, (sq_h[c][:, here], sq_l[c][:, here]))
            out[c, :, here] = 0.5 * (part_eye[:, here] - (1.5 * rows_of[c]["x1"][:, here] - 0.5 * y3))
            copies.append(
                pltpu.make_async_copy(out.at[c, :, here], target.at[c, :, here], sent.at[c, index])
            )
            copies[-1].start()

    stages = [
        squared,
        scaled,
        start,
        lambda c: step(c, "x1", "y1"),
        lambda c: step(c, "y1", "y2"),
        finish,
    ]
    for index in range(len(stages) + cols - 1):
        for c in columns:
            if 0 <= index - c < len(stages):
                stages[index - c](c)
    for copy in copies:
        copy.wait()


def column_kernel(cols, reach, rep_size, even, mask, fermi, place, *refs):
    inputs = 3 * rep_size
    pieces, (kept, far, target) = refs[:inputs], refs[inputs : inputs + 3]
    root, scratch = refs[inputs + 3 : inputs + 12], refs[inputs + 12 :]
    root_kernel(cols, reach, rep_size, even, mask, *pieces, *root)
    density_kernel(
        cols, reach, rep_size, even, mask, fermi, place,
        *root, kept, far, pieces[2 * rep_size], target, *scratch,
    )


def two_sided(one, block):
    return jnp.where(upper(block), 0.0, one.T)


def shaped(*shape, dtype=F32):
    return jax.ShapeDtypeStruct(shape, dtype)


SMEM = pl.BlockSpec(memory_space=pltpu.SMEM)
VMEM = pl.BlockSpec(memory_space=pltpu.VMEM)


def edges(even, mask, band, own):
    cols, count, block, _ = band.shape
    reach = (count - 1) // 2
    cross = len(crossing(reach))
    height = (2 + cross) * block + TILE
    return pl.pallas_call(
        functools.partial(edge_kernel, reach),
        out_shape=[shaped(height, block), shaped(height + own.shape[0] * own.shape[1], block), shaped(3 + 2 * cross, block, block), shaped(cols, *own.shape[1:]), shaped(*mask.shape)],
        in_specs=[SMEM, VMEM, VMEM, VMEM],
        out_specs=[VMEM] * 5,
        compiler_params=pltpu.CompilerParams(vmem_limit_bytes=8 * 2**20),
        cost_estimate=pl.CostEstimate(flops=0, bytes_accessed=4 * 2**20, transcendentals=0),
    )(even, mask, band, own)


def density(even, mask, fermi, place, owns, fars, nears, kept, far, reach):
    rep_size = len(owns)
    cols, piece, block = owns[0].shape
    depth = piece * rep_size
    width = (2 * reach + 1) * block
    rows = width // rep_size
    window = (cols + 2 * reach) * block
    return pl.pallas_call(
        functools.partial(column_kernel, cols, reach, rep_size),
        out_shape=shaped(cols, rows, width),
        in_specs=[SMEM, VMEM, SMEM, SMEM] + [VMEM] * (3 * rep_size + 2),
        out_specs=pl.BlockSpec(memory_space=pl.ANY),
        scratch_shapes=[
            *[pltpu.VMEM((cols, depth, width), BF16)] * 2,
            *[pltpu.VMEM((cols, width, depth), BF16)] * 2,
            *[pltpu.VMEM((cols, depth, width), BF16)] * 2,
            *[pltpu.VMEM((cols, width, depth), BF16)] * 2,
            pltpu.VMEM((cols, TILE, block), F32),
            pltpu.VMEM((window, window), F32),
            pltpu.VMEM((window, window), BF16),
            pltpu.VMEM((window, window), BF16),
            pltpu.VMEM((cols, width, width) if rows % PACKED else (1, TILE, block), F32),
            pltpu.VMEM((cols, rows, width), F32),
            pltpu.SemaphoreType.DMA((cols, pl.cdiv(width, STEP))),
            *[pltpu.VMEM((width, width), F32)] * cols,
            *[pltpu.VMEM((width, width), BF16)] * (4 * cols),
            *[pltpu.VMEM((width, depth), F32)] * cols,
            *[pltpu.VMEM((width, depth), BF16)] * (2 * cols),
            *[pltpu.VMEM((block, width), F32)] * cols,
        ],
        compiler_params=pltpu.CompilerParams(vmem_limit_bytes=36 * 2**20),
        cost_estimate=pl.CostEstimate(flops=2**34, bytes_accessed=8 * 2**20, transcendentals=0),
    )(even, mask, fermi, place, *owns, *fars, *nears, kept, far)


def near_swap(value):
    return lax.ppermute(value, "cols", [(i, i ^ 1) for i in range(lax.axis_size("cols"))])


def far_swap(value):
    count = lax.axis_size("cols")
    return lax.ppermute(value, "cols", [(i, (((i + 1) ^ 1) - 1) % count) for i in range(count)])


def rep_swap(value, step):
    return lax.ppermute(value, "rep", [(i, i ^ step) for i in range(lax.axis_size("rep"))])


def on_device(hamiltonian_band, margin_factors, neighbour_mask, fermi_level):
    cols, count, _, _ = hamiltonian_band.shape
    reach = (count - 1) // 2
    rep_size = lax.axis_size("rep")
    even = 1 - (lax.axis_index("cols").astype(jnp.int32) % 2).reshape(1)
    place = lax.axis_index("rep").astype(jnp.int32).reshape(1)
    margin_far = far_swap(margin_factors)
    to_far, to_near, kept, own, flags = edges(even, neighbour_mask, hamiltonian_band, margin_factors)
    far = far_swap(to_far)
    near = near_swap(to_near)
    group = jnp.concatenate([own, margin_far], axis=0)
    groups = [group] + [rep_swap(group, step) for step in range(1, rep_size)]
    owns = [own] + groups[1:]
    fars = [margin_far] + groups[1:]
    nears = [near] + [near_swap(value) for value in groups[1:]]
    return density(even, flags, fermi_level, place, owns, fars, nears, kept, far, reach)


def solution(mesh):
    in_specs = (P("cols", None, None, None), P("cols", "rep", None), P("cols", None), P())
    out_specs = P("cols", "rep", None)
    return jax.shard_map(
        on_device, mesh=mesh, in_specs=in_specs, out_specs=out_specs, check_vma=False
    )
```
